32 devices in a mesh: node: 16 (over z, x, core), local: 2 (over y).
Axes of the slice: x: 2, y: 2, z: 4, core: 2. Of those that a mesh axis runs over, the one named last changes fastest.
Arguments:
- hidden_in: bfloat16 [6144, 14848], P(('node', 'local')), may hold values from -6 to 6
- grad_heads: bfloat16 [6144, 192], P(('node', 'local')), may hold values from -6 to 6
- w_qkv: bfloat16 [14848, 320], P(('local', 'node'))
- ln_gain: bfloat16 [14848], P(('local', 'node')), may hold values from 0.099609375 to 1.8984375
- ln_bias: bfloat16 [14848], P(('local', 'node')), may hold values from -3 to 3
- seq_lengths: int32 [16], P('node'), may hold values from 96 to 384, as said below
- sample_index: int32 [16], P('node'), may hold values from 0 to 8191
- priority: float32 [8192], replicated, may hold values from 0.25 to 4
Outputs:
- grad_input: bfloat16 [6144, 14848], P(('node', 'local'))
- grad_qkv: float32 [14848, 320], P(('local', 'node'))
- grad_gain: float32 [14848], P(('local', 'node'))
- grad_bias: float32 [14848], P(('local', 'node'))
The draws below stay inside these ranges and needn't reach their ends.
Inputs may be any that keep to these rules, and one draw needn't show every extreme that they name: `seq_lengths`: exactly 384 for at least one sequence in every draw.
All inputs are finite; a program needn't handle non-finite values.
Results may differ from the reference program's by a relative error of at most 0.02.
The reference program's roundings to bfloat16 on the way count: a program that leaves them out, or rounds other values in their place, can miss the bound.
Values may be sent and summed in bfloat16 or wider, within the bound.
A program may use at most 128 MiB of HBM per device.

```python
import math
import jax
import jax.numpy as jnp
from jax import lax

D = 14848
HD = 64
QH = 3
QKV = 320
TOK_DEV = 192
LEN = 384
SEQS = 16
TOKENS = 6144
BUFFER = 8192


def draw_w_qkv(key, part):
    key = jax.random.fold_in(key, 11)
    entries = jax.random.normal(key, (D, QKV), jnp.float32) * D ** (-0.5)
    return entries.astype(jnp.bfloat16)


def draw_seq_lengths(key, part):
    key = jax.random.fold_in(key, 5)
    draw_key, pick_key = jax.random.split(key)
    lengths = jax.random.randint(draw_key, (SEQS,), LEN // 4, LEN + 1, dtype=jnp.int32)
    chosen = jax.random.randint(pick_key, (), 0, SEQS, dtype=jnp.int32)
    return jnp.where(jnp.arange(SEQS) == chosen, LEN, lengths).astype(jnp.int32)


def place_ends(array, key, least, top_value):
    longest = array.shape.index(max(array.shape))
    spots = []
    for shift in (0, 1):
        where = [jax.random.randint(jax.random.fold_in(key, axis), (), 0, length) for axis, length in enumerate(array.shape)]
        where[longest] = (where[longest] + shift) % array.shape[longest]
        spots.append(tuple(where))
    return array.at[spots[0]].set(least).at[spots[1]].set(top_value)


def block_levels(own_key, dims, pieces, least, top_value):
    level = 1.0
    for axis_at, shards_of in pieces:
        steps = jax.random.uniform(jax.random.fold_in(jax.random.fold_in(own_key, 6), axis_at), (shards_of,), jnp.float32, least / len(pieces), top_value / len(pieces))
        level = level * jnp.repeat(jnp.exp(steps), dims[axis_at] // shards_of).reshape((-1,) + (1,) * (len(dims) - 1 - axis_at))
    return level


def normal_values(stream_key, extent, scale, reach, shards=(), kind=jnp.bfloat16):
    factor_of = block_levels(stream_key, extent, shards, -0.22, 0.18) if shards else 1.0
    drawn = jax.random.normal(stream_key, extent, jnp.float32) * scale * factor_of
    return jnp.minimum(jnp.maximum(drawn, -reach), reach).astype(kind)


def setup_inputs(seed: int = 0) -> dict:
    key_list = jax.random.split(jax.random.key(seed), 9)
    hidden_in = normal_values(key_list[0], (TOKENS, D), 1.0, 6.0, ((0, 32),))
    grad_heads = normal_values(key_list[1], (TOKENS, QH * HD), 1.0, 6.0, ((0, 32),))
    w_qkv = draw_w_qkv(jax.random.fold_in(key_list[8], 71), 0)
    ln_gain = jnp.clip(1.0 + 0.18 * jax.random.normal(key_list[3], (D,), jnp.float32), 0.099609375, 1.8984375).astype(jnp.bfloat16)
    ln_bias = normal_values(key_list[4], (D,), 0.5, 3.0, ((0, 32),))
    seq_lengths = draw_seq_lengths(jax.random.fold_in(key_list[8], 71), 0)
    sample_index = place_ends(jax.random.randint(key_list[6], (SEQS,), 0, BUFFER), jax.random.fold_in(key_list[6], 1), 0, BUFFER - 1).astype(jnp.int32)
    priority = jnp.clip(jnp.exp(jax.random.uniform(key_list[7], (BUFFER,), jnp.float32, math.log(0.25), math.log(4.0))), 0.25, 4.0)
    return dict(hidden_in=hidden_in, grad_heads=grad_heads, w_qkv=w_qkv, ln_gain=ln_gain, ln_bias=ln_bias, seq_lengths=seq_lengths, sample_index=sample_index, priority=priority)


epsilon = 1e-05

def layer_stats(hidden):
    values = hidden.astype(jnp.float32)
    centre = lax.optimization_barrier(jnp.mean(values, axis=-1, keepdims=True))
    shifted = values - centre
    variance = lax.optimization_barrier(jnp.mean(shifted * shifted, axis=-1, keepdims=True))
    inverse = lax.rsqrt(variance + epsilon)
    return (shifted * inverse, inverse)

def rope_tables(positions, head_size):
    half_size = head_size // 2
    steps = 2.0 * jnp.arange(half_size, dtype=jnp.float32) / head_size
    freqs = jnp.exp(-jnp.log(10000.0) * steps)
    angles = positions.astype(jnp.float32)[:, None] * freqs[None, :]
    cosine = jnp.concatenate([jnp.cos(angles), jnp.cos(angles)], axis=1)
    sine_table = jnp.concatenate([jnp.sin(angles), jnp.sin(angles)], axis=1)
    return (cosine, sine_table)

def rotate(values, cosine, sine_table):
    half_size = values.shape[-1] // 2
    turned = jnp.concatenate([-values[..., half_size:], values[..., :half_size]], axis=-1)
    return values * cosine[:, None, :] + turned * sine_table[:, None, :]

def unrotate(values, cosine, sine_table):
    half_size = values.shape[-1] // 2
    turned = jnp.concatenate([values[..., half_size:], -values[..., :half_size]], axis=-1)
    return values * cosine[:, None, :] + turned * sine_table[:, None, :]

def block_round(terms):
    rounded = lax.optimization_barrier(terms.astype(jnp.bfloat16))
    return lax.optimization_barrier(jnp.sum(rounded.astype(jnp.float32), axis=0))

def one_sequence(hidden, cotangent_in, length, weight, w_qkv, ln_gain, ln_bias):
    seq_rows = hidden.shape[0]
    model_width = hidden.shape[1]
    query_cols = QH * HD
    normalized, inverse = layer_stats(hidden)
    normed = (normalized * ln_gain.astype(jnp.float32) + ln_bias.astype(jnp.float32)).astype(jnp.bfloat16)
    projected = jnp.dot(normed, w_qkv, preferred_element_type=jnp.float32)
    positions = jnp.arange(seq_rows, dtype=jnp.int32)
    cosine, sine_table = rope_tables(positions, HD)
    query = rotate(projected[:, :query_cols].reshape(seq_rows, QH, HD), cosine, sine_table).astype(jnp.bfloat16)
    keys_all = rotate(projected[:, query_cols:query_cols + HD][:, None, :], cosine, sine_table)[:, 0, :].astype(jnp.bfloat16)
    values_all = projected[:, query_cols + HD:].astype(jnp.bfloat16)
    scale = HD ** (-0.5)
    scores = jnp.einsum('qhd,kd->hqk', query.astype(jnp.float32), keys_all.astype(jnp.float32)) * scale
    allowed = (positions[None, :] <= positions[:, None]) & (positions[None, :] < length)
    scores = jnp.where(allowed[None], scores, -1e+30)
    row_max = lax.optimization_barrier(jnp.max(scores, axis=-1, keepdims=True))
    exponent = jnp.exp(scores - row_max)
    attention = exponent / lax.optimization_barrier(jnp.sum(exponent, axis=-1, keepdims=True))
    attention_b = attention.astype(jnp.bfloat16)
    head_out = jnp.einsum('hqk,kd->qhd', attention_b.astype(jnp.float32), values_all.astype(jnp.float32))
    live_rows = (positions < length).astype(jnp.float32)
    cotangent = (cotangent_in.reshape(seq_rows, QH, HD).astype(jnp.float32) * weight * live_rows[:, None, None]).astype(jnp.bfloat16)
    cot_wide = cotangent.astype(jnp.float32)
    d_attention = jnp.einsum('qhd,kd->hqk', cot_wide, values_all.astype(jnp.float32))
    row_delta = lax.optimization_barrier(jnp.sum(cot_wide * head_out, axis=-1))
    d_scores = (attention * (d_attention - row_delta.T[:, :, None]) * scale).astype(jnp.bfloat16)
    d_wide = d_scores.astype(jnp.float32)
    d_query = jnp.einsum('hqk,kd->qhd', d_wide, keys_all.astype(jnp.float32))
    d_key = jnp.einsum('hqk,qhd->kd', d_wide, query.astype(jnp.float32))
    d_value = jnp.einsum('hqk,qhd->kd', attention_b.astype(jnp.float32), cot_wide)
    d_query_pre = unrotate(d_query, cosine, sine_table).reshape(seq_rows, query_cols)
    d_key_pre = unrotate(d_key[:, None, :], cosine, sine_table)[:, 0, :]
    d_projected = jnp.concatenate([d_query_pre, d_key_pre, d_value], axis=1).astype(jnp.bfloat16)
    d_normed = jnp.dot(d_projected, w_qkv.T, preferred_element_type=jnp.float32)
    grad_hat = d_normed * ln_gain.astype(jnp.float32)
    grad_input = inverse * (grad_hat - lax.optimization_barrier(jnp.mean(grad_hat, axis=-1, keepdims=True)) - normalized * lax.optimization_barrier(jnp.mean(grad_hat * normalized, axis=-1, keepdims=True)))
    blocks = seq_rows // TOK_DEV
    normed_blocks = normed.reshape(blocks, TOK_DEV, model_width).astype(jnp.float32)
    proj_blocks = d_projected.reshape(blocks, TOK_DEV, QKV).astype(jnp.float32)
    part_weight = block_round(jnp.einsum('btd,btc->bdc', normed_blocks, proj_blocks))
    part_gain = block_round(lax.optimization_barrier(jnp.sum((d_normed * normalized).reshape(blocks, TOK_DEV, model_width), axis=1)))
    part_bias = block_round(lax.optimization_barrier(jnp.sum(d_normed.reshape(blocks, TOK_DEV, model_width), axis=1)))
    return (grad_input.astype(jnp.bfloat16), part_weight, part_gain, part_bias)

def reference(hidden_in, grad_heads, w_qkv, ln_gain, ln_bias, seq_lengths, sample_index, priority):
    hidden_seq = hidden_in.reshape(SEQS, LEN, D)
    grad_seq = grad_heads.reshape(SEQS, LEN, QH * HD)
    importance = priority[sample_index]
    start = (jnp.zeros((D, QKV), jnp.float32), jnp.zeros((D,), jnp.float32), jnp.zeros((D,), jnp.float32))

    def advance(carry, items):
        hidden, cotangent_in, length, weight = items
        grad_x, part_weight, part_gain, part_bias = one_sequence(hidden, cotangent_in, length, weight, w_qkv, ln_gain, ln_bias)
        return ((carry[0] + part_weight, carry[1] + part_gain, carry[2] + part_bias), grad_x)
    totals, grad_rows = lax.scan(advance, start, (hidden_seq, grad_seq, seq_lengths, importance))
    return (grad_rows.reshape(TOKENS, D), totals[0], totals[1], totals[2])
```

```python
import functools

import jax
import jax.numpy as jnp
from jax import lax
from jax.experimental import pallas as pl
from jax.experimental.pallas import tpu as pltpu
from jax.sharding import PartitionSpec as P

HD = 64
QH = 3
LANES = 384
MESH = pl.DeviceIdType.MESH


epsilon = 1e-05


def rope_tables(positions, head_size):
    half_size = head_size // 2
    steps = 2.0 * jnp.arange(half_size, dtype=jnp.float32) / head_size
    freqs = jnp.exp(-jnp.log(10000.0) * steps)
    angles = positions.astype(jnp.float32)[:, None] * freqs[None, :]
    cosine = jnp.concatenate([jnp.cos(angles), jnp.cos(angles)], axis=1)
    sine_table = jnp.concatenate([jnp.sin(angles), jnp.sin(angles)], axis=1)
    return (cosine, sine_table)


def rotate(values, cosine, sine_table):
    half_size = values.shape[-1] // 2
    turned = jnp.concatenate([-values[..., half_size:], values[..., :half_size]], axis=-1)
    return values * cosine[:, None, :] + turned * sine_table[:, None, :]


def unrotate(values, cosine, sine_table):
    half_size = values.shape[-1] // 2
    turned = jnp.concatenate([values[..., half_size:], -values[..., :half_size]], axis=-1)
    return values * cosine[:, None, :] + turned * sine_table[:, None, :]


def place(Z, L):
    node = lax.axis_index("node")
    z, x, c = node // 4, (node // 2) % 2, node % 2
    q = lax.axis_index("local") * 2 + x
    return z, q, c


def device(z, q, c):
    return (z * 4 + (q % 2) * 2 + c, q // 2)


def greet(Z, Q, z, q, c):
    barrier = pltpu.get_barrier_semaphore()

    def tell(target):
        pl.semaphore_signal(barrier, inc=1, device_id=target, device_id_type=MESH)

    tell(device(z, q, 1 - c))
    for d in range(1, Z):
        tell(device((z + d) % Z, q, c))
    for d in range(1, Q):
        tell(device(z, (q + d) % Q, c))
    pl.semaphore_wait(barrier, Z + Q - 1)


def gather_kernel(Z, L, own, out, local_sem, send_z, send_q, send_c, recv, recv_c):
    Q = 2 * L
    z, q, c = place(Z, L)
    greet(Z, Q, z, q, c)

    def remote(src, zz, qq, send, got, target):
        return pltpu.make_async_remote_copy(
            src_ref=src,
            dst_ref=out.at[qq, zz, c],
            send_sem=send,
            recv_sem=got,
            device_id=target,
            device_id_type=MESH,
        )

    mine = pltpu.make_async_copy(own, out.at[q, z, c], local_sem)
    mine.start()

    def to_z(d):
        return remote(own, z, q, send_z.at[d - 1], recv.at[q, z], device((z + d) % Z, q, c))

    def to_q(k, d, src):
        zz = (z + Z - k) % Z
        return remote(src, zz, q, send_q.at[k, d - 1], recv.at[q, zz], device(z, (q + d) % Q, c))

    def to_c(zz, qq, src):
        return remote(src, zz, qq, send_c.at[qq, zz], recv_c.at[qq, zz], device(z, q, 1 - c))

    def landed(zz, qq):
        pltpu.make_async_copy(own, out.at[qq, zz, c], recv.at[qq, zz]).wait()

    for d in range(1, Z):
        to_z(d).start()
    for d in range(1, Q):
        to_q(0, d, own).start()
    to_c(z, q, own).start()

    def spread(k, carry):
        zz = (z + Z - k) % Z
        landed(zz, q)
        for d in range(1, Q):
            to_q(k, d, out.at[q, zz, c]).start()
        to_c(zz, q, out.at[q, zz, c]).start()
        return carry

    lax.fori_loop(1, Z, spread, 0)

    def forward(k, carry):
        zz = (z + Z - k) % Z
        for d in range(1, Q):
            qq = (q + d) % Q
            landed(zz, qq)
            to_c(zz, qq, out.at[qq, zz, c]).start()
        return carry

    lax.fori_loop(0, Z, forward, 0)

    mine.wait()
    for d in range(1, Z):
        to_z(d).wait_send()

    def finish(k, carry):
        for d in range(1, Q):
            to_q(k, d, own).wait_send()
        for d in range(Q):
            to_c(k, (q + d) % Q, own).wait_send()
            pltpu.make_async_copy(
                own, out.at[(q + d) % Q, k, 1 - c], recv_c.at[(q + d) % Q, k]
            ).wait()
        return carry

    lax.fori_loop(0, Z, finish, 0)


def gather(block, Z, L):
    rows = block.shape[0]
    Q = 2 * L
    return pl.pallas_call(
        functools.partial(gather_kernel, Z, L),
        out_shape=jax.ShapeDtypeStruct((Q, Z, 2, rows, LANES), jnp.bfloat16),
        in_specs=[pl.BlockSpec(memory_space=pl.ANY)],
        out_specs=pl.BlockSpec(memory_space=pl.ANY),
        scratch_shapes=[
            pltpu.SemaphoreType.DMA,
            pltpu.SemaphoreType.DMA((max(Z - 1, 1),)),
            pltpu.SemaphoreType.DMA((Z, Q - 1)),
            pltpu.SemaphoreType.DMA((Q, Z)),
            pltpu.SemaphoreType.DMA((Q, Z)),
            pltpu.SemaphoreType.DMA((Q, Z)),
        ],
        compiler_params=pltpu.CompilerParams(collective_id=0, has_side_effects=True),
    )(block)


def scatter_kernel(
    Z, L, part, out, own, pair, plane, tall, column,
    sem_own, send_c, recv_c, send_q, recv_q, send_z, recv_z,
):
    Q = 2 * L
    z, q, c = place(Z, L)
    greet(Z, Q, z, q, c)

    def load(zz, qq):
        return pltpu.make_async_copy(part.at[qq, zz, c], own.at[qq, zz], sem_own.at[qq, zz])

    def to_c(zz, qq):
        return pltpu.make_async_remote_copy(
            src_ref=part.at[qq, zz, 1 - c],
            dst_ref=pair.at[qq, zz],
            send_sem=send_c.at[qq, zz],
            recv_sem=recv_c.at[qq, zz],
            device_id=device(z, q, 1 - c),
            device_id_type=MESH,
        )

    def to_q(zz, qq):
        return pltpu.make_async_remote_copy(
            src_ref=own.at[qq, zz],
            dst_ref=plane.at[zz, q],
            send_sem=send_q.at[qq, zz],
            recv_sem=recv_q.at[zz, q],
            device_id=device(z, qq, c),
            device_id_type=MESH,
        )

    def to_z(zz):
        return pltpu.make_async_remote_copy(
            src_ref=tall.at[zz],
            dst_ref=column.at[z],
            send_sem=send_z.at[zz],
            recv_sem=recv_z.at[z],
            device_id=device(zz, q, c),
            device_id_type=MESH,
        )

    def begin(k, carry):
        zz = (z + k) % Z
        for d in range(Q):
            qq = (q + d + 1) % Q
            to_c(zz, qq).start()
            load(zz, qq).start()
        return carry

    lax.fori_loop(1, Z + 1, begin, 0)

    def join(zz, qq):
        load(zz, qq).wait()
        to_c(zz, qq).wait_recv()
        total = own[qq, zz].astype(jnp.float32) + pair[qq, zz].astype(jnp.float32)
        own[qq, zz] = total.astype(jnp.bfloat16)

    def pairs(k, carry):
        zz = (z + k) % Z

        def one(d, carry):
            qq = (q + d) % Q
            join(zz, qq)
            to_q(zz, qq).start()
            return carry

        lax.fori_loop(1, Q, one, 0)
        join(zz, q)
        return carry

    lax.fori_loop(1, Z + 1, pairs, 0)

    def plane_sum(zz):
        tall[zz] = own[q, zz].astype(jnp.float32)

        def add(d, carry):
            qq = (q + d) % Q
            pltpu.make_async_copy(own.at[qq, zz], plane.at[zz, qq], recv_q.at[zz, qq]).wait()
            tall[zz] += plane[zz, qq].astype(jnp.float32)
            return carry

        lax.fori_loop(1, Q, add, 0)

    def columns(k, carry):
        zz = (z + k) % Z
        plane_sum(zz)
        to_z(zz).start()
        return carry

    lax.fori_loop(1, Z, columns, 0)
    plane_sum(z)
    out[...] = tall[z]

    def last(k, carry):
        zz = (z + Z - k) % Z
        pltpu.make_async_copy(tall.at[zz], column.at[zz], recv_z.at[zz]).wait()
        out[...] += column[zz]
        return carry

    lax.fori_loop(1, Z, last, 0)

    def finish(k, carry):
        zz = (z + k) % Z
        for d in range(Q):
            to_c(zz, (q + d) % Q).wait_send()
        for d in range(1, Q):
            to_q(zz, (q + d) % Q).wait_send()
        return carry

    lax.fori_loop(0, Z, finish, 0)
    for d in range(1, Z):
        to_z((z + d) % Z).wait_send()


def scatter_sum(part, Z, L):
    rows = part.shape[-2]
    Q = 2 * L
    dma = pltpu.SemaphoreType.DMA
    return pl.pallas_call(
        functools.partial(scatter_kernel, Z, L),
        out_shape=jax.ShapeDtypeStruct((rows, LANES), jnp.float32),
        in_specs=[pl.BlockSpec(memory_space=pl.ANY)],
        out_specs=pl.BlockSpec(memory_space=pltpu.VMEM),
        scratch_shapes=[
            pltpu.VMEM((Q, Z, rows, LANES), jnp.bfloat16),
            pltpu.VMEM((Q, Z, rows, LANES), jnp.bfloat16),
            pltpu.VMEM((Z, Q, rows, LANES), jnp.bfloat16),
            pltpu.VMEM((Z, rows, LANES), jnp.float32),
            pltpu.VMEM((Z, rows, LANES), jnp.float32),
            dma((Q, Z)),
            dma((Q, Z)),
            dma((Q, Z)),
            dma((Q, Z)),
            dma((Z, Q)),
            dma((Z,)),
            dma((Z,)),
        ],
        compiler_params=pltpu.CompilerParams(
            collective_id=1, has_side_effects=True, vmem_limit_bytes=44 * 2**20
        ),
    )(part)


def on_device(
    Z, L, hidden_in, grad_heads, w_qkv, ln_gain, ln_bias, seq_lengths, sample_index, priority
):
    tok_rows, model_width = hidden_in.shape
    shard, qkv = w_qkv.shape
    padded = -(-shard // 16) * 16
    query_cols = QH * HD

    def whole(blocks):
        blocks = blocks[:, :, :, :shard]
        blocks = blocks.reshape((L, 2, Z, 2) + blocks.shape[3:])
        return blocks.transpose(0, 2, 1, 3, 4, 5).reshape(model_width, -1)

    def apart(rows):
        blocks = rows.reshape(L, Z, 2, 2, shard, -1).transpose(0, 2, 1, 3, 4, 5)
        blocks = blocks.reshape(2 * L, Z, 2, shard, -1)
        return jnp.pad(blocks, ((0, 0), (0, 0), (0, 0), (0, padded - shard), (0, 0)))

    own_block = jnp.concatenate([w_qkv, ln_gain[:, None], ln_bias[:, None]], axis=1)
    own_block = jnp.pad(own_block, ((0, padded - shard), (0, LANES - qkv - 2)))
    w_all = whole(gather(own_block, Z, L))
    picks = jnp.arange(16)[:, None] + qkv == jnp.arange(LANES)[None, :]
    picks = (picks & (jnp.arange(16) < 2)[:, None]).astype(jnp.bfloat16)
    contract = (((1,), (1,)), ((), ()))
    rows = lax.dot_general(picks, w_all, contract, preferred_element_type=jnp.float32)
    gain, bias = rows[0:1], rows[1:2]
    values = hidden_in.astype(jnp.float32)
    centre = jnp.mean(values, axis=-1, keepdims=True)
    shifted = values - centre
    variance = jnp.mean(shifted * shifted, axis=-1, keepdims=True)
    inverse = lax.rsqrt(variance + epsilon)
    normalized = shifted * inverse
    normed = (normalized * gain + bias).astype(jnp.bfloat16)
    proj_total = jnp.dot(normed, w_all, preferred_element_type=jnp.float32)[:, :qkv]
    positions = lax.axis_index("local") * tok_rows + jnp.arange(tok_rows, dtype=jnp.int32)
    cosine, sine_table = rope_tables(positions, HD)
    query = rotate(proj_total[:, :query_cols].reshape(tok_rows, QH, HD), cosine, sine_table).astype(
        jnp.bfloat16
    )
    keys_own = rotate(proj_total[:, query_cols : query_cols + HD][:, None, :], cosine, sine_table)[
        :, 0, :
    ]
    pair_own = jnp.concatenate([keys_own, proj_total[:, query_cols + HD :]], axis=1).astype(
        jnp.bfloat16
    )
    pair_all = lax.all_gather(pair_own, "local", axis=0, tiled=True)
    seq_rows = pair_all.shape[0]
    keys_all = pair_all[:, :HD]
    values_all = pair_all[:, HD:]
    length = seq_lengths[0]
    weight = lax.dynamic_slice(priority, (sample_index[0],), (1,))[0]
    scale = HD ** (-0.5)
    scores = jnp.einsum("qhd,kd->hqk", query, keys_all, preferred_element_type=jnp.float32) * scale
    key_positions = jnp.arange(seq_rows, dtype=jnp.int32)
    allowed = (key_positions[None, :] <= positions[:, None]) & (key_positions[None, :] < length)
    scores = jnp.where(allowed[None], scores, -1e30)
    row_max = jnp.max(scores, axis=-1, keepdims=True)
    exponent = jnp.exp(scores - row_max)
    attention = exponent / jnp.sum(exponent, axis=-1, keepdims=True)
    attention_b = attention.astype(jnp.bfloat16)
    head_out = jnp.einsum(
        "hqk,kd->qhd", attention_b, values_all, preferred_element_type=jnp.float32
    )
    live_rows = (positions < length).astype(jnp.float32)
    cotangent = (
        grad_heads.reshape(tok_rows, QH, HD).astype(jnp.float32) * weight * live_rows[:, None, None]
    ).astype(jnp.bfloat16)
    d_attention = jnp.einsum(
        "qhd,kd->hqk", cotangent, values_all, preferred_element_type=jnp.float32
    )
    row_delta = jnp.sum(cotangent.astype(jnp.float32) * head_out, axis=-1)
    d_scores = (attention * (d_attention - row_delta.T[:, :, None]) * scale).astype(jnp.bfloat16)
    d_query = jnp.einsum("hqk,kd->qhd", d_scores, keys_all, preferred_element_type=jnp.float32)
    d_key_term = jnp.einsum("hqk,qhd->kd", d_scores, query, preferred_element_type=jnp.float32)
    d_value_term = jnp.einsum(
        "hqk,qhd->kd", attention_b, cotangent, preferred_element_type=jnp.float32
    )
    d_pair = lax.psum_scatter(
        jnp.concatenate([d_key_term, d_value_term], axis=1),
        "local",
        scatter_dimension=0,
        tiled=True,
    )
    d_query_pre = unrotate(d_query, cosine, sine_table).reshape(tok_rows, query_cols)
    d_key_pre = unrotate(d_pair[:, None, :HD], cosine, sine_table)[:, 0, :]
    d_projected = jnp.concatenate([d_query_pre, d_key_pre, d_pair[:, HD:]], axis=1)
    d_projected = jnp.pad(d_projected.astype(jnp.bfloat16), ((0, 0), (0, LANES - qkv)))
    d_normed = lax.dot_general(d_projected, w_all, contract, preferred_element_type=jnp.float32)
    grad_hat = d_normed * gain
    grad_input = inverse * (
        grad_hat
        - jnp.mean(grad_hat, axis=-1, keepdims=True)
        - normalized * jnp.mean(grad_hat * normalized, axis=-1, keepdims=True)
    )
    term_gain = jnp.sum(d_normed * normalized, axis=0, keepdims=True).astype(jnp.bfloat16)
    term_bias = jnp.sum(d_normed, axis=0, keepdims=True).astype(jnp.bfloat16)
    left = jnp.concatenate(
        [normed, term_gain, term_bias, jnp.zeros((14, model_width), jnp.bfloat16)], axis=0
    )
    right = jnp.concatenate([d_projected, picks], axis=0)
    term = lax.dot_general(
        left, right, (((0,), (0,)), ((), ())), preferred_element_type=jnp.float32
    ).astype(jnp.bfloat16)
    totals = scatter_sum(apart(term), Z, L)[:shard]
    return (
        grad_input.astype(jnp.bfloat16),
        totals[:, :qkv],
        totals[:, qkv],
        totals[:, qkv + 1],
    )


def solution(mesh):
    Z, L = mesh.shape["node"] // 4, mesh.shape["local"]
    return jax.shard_map(
        functools.partial(on_device, Z, L),
        mesh=mesh,
        in_specs=(
            P(("node", "local"), None),
            P(("node", "local"), None),
            P(("local", "node"), None),
            P(("local", "node")),
            P(("local", "node")),
            P("node"),
            P("node"),
            P(),
        ),
        out_specs=(
            P(("node", "local"), None),
            P(("local", "node"), None),
            P(("local", "node")),
            P(("local", "node")),
        ),
        check_vma=False,
    )
```

```python
import functools

import jax
import jax.numpy as jnp
from jax import lax
from jax.experimental import pallas as pl
from jax.experimental.pallas import tpu as pltpu
from jax.sharding import PartitionSpec as P

HD = 64
QH = 3
LANES = 384
MESH = pl.DeviceIdType.MESH


epsilon = 1e-05


def rope_tables(positions, head_size):
    half_size = head_size // 2
    steps = 2.0 * jnp.arange(half_size, dtype=jnp.float32) / head_size
    freqs = jnp.exp(-jnp.log(10000.0) * steps)
    angles = positions.astype(jnp.float32)[:, None] * freqs[None, :]
    cosine = jnp.concatenate([jnp.cos(angles), jnp.cos(angles)], axis=1)
    sine_table = jnp.concatenate([jnp.sin(angles), jnp.sin(angles)], axis=1)
    return (cosine, sine_table)


def rotate(values, cosine, sine_table):
    half_size = values.shape[-1] // 2
    turned = jnp.concatenate([-values[..., half_size:], values[..., :half_size]], axis=-1)
    return values * cosine[:, None, :] + turned * sine_table[:, None, :]


def unrotate(values, cosine, sine_table):
    half_size = values.shape[-1] // 2
    turned = jnp.concatenate([values[..., half_size:], -values[..., :half_size]], axis=-1)
    return values * cosine[:, None, :] + turned * sine_table[:, None, :]


def place(Z, L):
    node = lax.axis_index("node")
    z, x, c = node // 4, (node // 2) % 2, node % 2
    q = lax.axis_index("local") * 2 + x
    return z, q, c


def device(z, q, c):
    return (z * 4 + (q % 2) * 2 + c, q // 2)


def greet(Z, Q, z, q, c):
    barrier = pltpu.get_barrier_semaphore()

    def tell(target):
        pl.semaphore_signal(barrier, inc=1, device_id=target, device_id_type=MESH)

    tell(device(z, q, 1 - c))
    for d in range(1, Z):
        tell(device((z + d) % Z, q, c))
    for d in range(1, Q):
        tell(device(z, (q + d) % Q, c))
    pl.semaphore_wait(barrier, Z + Q - 1)


def gather_kernel(
    Z, L, own, hidden, out, centre, variance, held,
    local_sem, send_z, send_x, send_y, send_r0, send_r1, send_c,
    recv, recv_0, recv_1, recv_c,
):
    Q = 2 * L
    rows = own.shape[0]
    half = -(-(rows // 2) // 16) * 16
    z, q, c = place(Z, L)
    l, x = q // 2, q % 2
    greet(Z, Q, z, q, c)

    def block(zz, qq):
        return out.at[qq // 2, zz, qq % 2, c]

    def remote(src, dst, send, got, target):
        return pltpu.make_async_remote_copy(
            src_ref=src, dst_ref=dst, send_sem=send, recv_sem=got,
            device_id=target, device_id_type=MESH,
        )

    across = q + 1 - 2 * x

    def beside(d):
        return ((l + d) % L) * 2 + x

    mine = pltpu.make_async_copy(own, block(z, q), local_sem.at[0])
    mine.start()
    fetch = pltpu.make_async_copy(hidden, held, local_sem.at[1])
    fetch.start()

    def to_z(d):
        return remote(
            own, block(z, q), send_z.at[d - 1], recv.at[q, z], device((z + d) % Z, q, c)
        )

    def to_x(zz, src):
        return remote(src, block(zz, q), send_x.at[zz], recv.at[q, zz], device(z, across, c))

    def to_y(zz, d, src):
        return remote(
            src, block(zz, q), send_y.at[zz, d - 1], recv.at[q, zz], device(z, beside(d), c)
        )

    def relay_x(zz, d):
        part = block(zz, beside(d)).at[pl.ds(0, half)]
        return remote(
            part, part, send_r0.at[zz, d - 1], recv_0.at[beside(d), zz], device(z, across, c)
        )

    def relay_y(zz, d):
        part = block(zz, across).at[pl.ds(half, rows - half)]
        return remote(
            part, part, send_r1.at[zz, d - 1], recv_1.at[across, zz], device(z, beside(d), c)
        )

    def to_c(zz, qq, src):
        return remote(src, block(zz, qq), send_c.at[qq, zz], recv_c.at[qq, zz], device(z, q, 1 - c))

    def landed(zz, qq):
        pltpu.make_async_copy(own, block(zz, qq), recv.at[qq, zz]).wait()

    for d in range(1, Z):
        to_z(d).start()
    to_x(z, own).start()
    for d in range(1, L):
        to_y(z, d, own).start()
    to_c(z, q, own).start()

    fetch.wait()
    width = held.shape[1]

    def stats(g, carry):
        span = pl.ds(pl.multiple_of(g * 16, 16), 16)
        mean = jnp.sum(held[span, :].astype(jnp.float32), axis=1, keepdims=True) / width
        shifted = held[span, :].astype(jnp.float32) - mean
        spread_of = jnp.sum(shifted * shifted, axis=1, keepdims=True) / width
        centre[span, :] = jnp.broadcast_to(mean, (16, 128))
        variance[span, :] = jnp.broadcast_to(spread_of, (16, 128))
        return carry

    lax.fori_loop(0, held.shape[0] // 16, stats, 0)

    def spread(k):
        zz = (z + Z - k) % Z
        landed(zz, q)
        to_x(zz, block(zz, q)).start()
        for d in range(1, L):
            to_y(zz, d, block(zz, q)).start()
        to_c(zz, q, block(zz, q)).start()

    def relay(k):
        zz = (z + Z - k) % Z
        landed(zz, across)
        for d in range(1, L):
            relay_y(zz, d).start()
        to_c(zz, across, block(zz, across)).start()
        for d in range(1, L):
            landed(zz, beside(d))
            relay_x(zz, d).start()
            to_c(zz, beside(d), block(zz, beside(d))).start()

    def middle(k, carry):
        spread(k)
        relay(k - 1)
        return carry

    lax.fori_loop(1, Z, middle, 0)
    relay(Z - 1)

    def corners(k, carry):
        zz = (z + Z - k) % Z
        for d in range(1, L):
            qq = beside(d) + 1 - 2 * x
            at = block(zz, qq)
            low, high = pl.ds(0, half), pl.ds(half, rows - half)
            pltpu.make_async_copy(own.at[low], at.at[low], recv_0.at[qq, zz]).wait()
            pltpu.make_async_copy(own.at[high], at.at[high], recv_1.at[qq, zz]).wait()
            to_c(zz, qq, at).start()
        return carry

    lax.fori_loop(0, Z, corners, 0)

    mine.wait()
    for d in range(1, Z):
        to_z(d).wait_send()

    def finish(k, carry):
        to_x(k, own).wait_send()
        for d in range(1, L):
            to_y(k, d, own).wait_send()
            relay_x(k, d).wait_send()
            relay_y(k, d).wait_send()
        for d in range(Q):
            qq = (q + d) % Q
            to_c(k, qq, own).wait_send()
            pltpu.make_async_copy(own, out.at[qq // 2, k, qq % 2, 1 - c], recv_c.at[qq, k]).wait()
        return carry

    lax.fori_loop(0, Z, finish, 0)


def gather(block, hidden, Z, L):
    rows = block.shape[0]
    tokens = hidden.shape[0]
    Q = 2 * L
    dma = pltpu.SemaphoreType.DMA
    others = max(L - 1, 1)
    return pl.pallas_call(
        functools.partial(gather_kernel, Z, L),
        out_shape=(
            jax.ShapeDtypeStruct((L, Z, 2, 2, rows, LANES), jnp.bfloat16),
            jax.ShapeDtypeStruct((tokens, 128), jnp.float32),
            jax.ShapeDtypeStruct((tokens, 128), jnp.float32),
        ),
        in_specs=[pl.BlockSpec(memory_space=pl.ANY)] * 2,
        out_specs=(
            pl.BlockSpec(memory_space=pl.ANY),
            pl.BlockSpec(memory_space=pltpu.VMEM),
            pl.BlockSpec(memory_space=pltpu.VMEM),
        ),
        scratch_shapes=[
            pltpu.VMEM(hidden.shape, jnp.bfloat16),
            dma((2,)),
            dma((max(Z - 1, 1),)),
            dma((Z,)),
            dma((Z, others)),
            dma((Z, others)),
            dma((Z, others)),
            dma((Q, Z)),
            dma((Q, Z)),
            dma((Q, Z)),
            dma((Q, Z)),
            dma((Q, Z)),
        ],
        compiler_params=pltpu.CompilerParams(
            collective_id=0, has_side_effects=True, vmem_limit_bytes=32 * 2**20
        ),
    )(block, hidden)


def scatter_kernel(
    Z, L, part, out, own, pair, plane, tall, column,
    sem_own, send_c, recv_c, send_q, recv_q, send_z, recv_z,
):
    Q = 2 * L
    z, q, c = place(Z, L)
    greet(Z, Q, z, q, c)

    def load(zz, qq):
        return pltpu.make_async_copy(part.at[qq // 2, zz, qq % 2, c], own.at[qq, zz], sem_own.at[qq, zz])

    def to_c(zz, qq):
        return pltpu.make_async_remote_copy(
            src_ref=part.at[qq // 2, zz, qq % 2, 1 - c],
            dst_ref=pair.at[qq, zz],
            send_sem=send_c.at[qq, zz],
            recv_sem=recv_c.at[qq, zz],
            device_id=device(z, q, 1 - c),
            device_id_type=MESH,
        )

    def to_q(zz, qq):
        return pltpu.make_async_remote_copy(
            src_ref=own.at[qq, zz],
            dst_ref=plane.at[zz, q],
            send_sem=send_q.at[qq, zz],
            recv_sem=recv_q.at[zz, q],
            device_id=device(z, qq, c),
            device_id_type=MESH,
        )

    def to_z(zz):
        return pltpu.make_async_remote_copy(
            src_ref=tall.at[zz],
            dst_ref=column.at[z],
            send_sem=send_z.at[zz],
            recv_sem=recv_z.at[z],
            device_id=device(zz, q, c),
            device_id_type=MESH,
        )

    def begin(k, carry):
        zz = (z + k) % Z
        for d in range(Q):
            qq = (q + d + 1) % Q
            to_c(zz, qq).start()
            load(zz, qq).start()
        return carry

    lax.fori_loop(1, Z + 1, begin, 0)

    def join(zz, qq):
        load(zz, qq).wait()
        to_c(zz, qq).wait_recv()
        total = own[qq, zz].astype(jnp.float32) + pair[qq, zz].astype(jnp.float32)
        own[qq, zz] = total.astype(jnp.bfloat16)

    def pairs(k):
        zz = (z + k) % Z

        def one(d, carry):
            qq = (q + d) % Q
            join(zz, qq)
            to_q(zz, qq).start()
            return carry

        lax.fori_loop(1, Q, one, 0)
        join(zz, q)

    pairs(1)

    def plane_sum(zz):
        tall[zz] = own[q, zz].astype(jnp.float32)

        def add(d, carry):
            qq = (q + d) % Q
            pltpu.make_async_copy(own.at[qq, zz], plane.at[zz, qq], recv_q.at[zz, qq]).wait()
            tall[zz] += plane[zz, qq].astype(jnp.float32)
            return carry

        lax.fori_loop(1, Q, add, 0)

    def columns(k, carry):
        pairs(k + 1)
        zz = (z + k) % Z
        plane_sum(zz)
        to_z(zz).start()
        return carry

    lax.fori_loop(1, Z, columns, 0)
    plane_sum(z)
    out[...] = tall[z]

    def last(k, carry):
        zz = (z + Z - k) % Z
        pltpu.make_async_copy(tall.at[zz], column.at[zz], recv_z.at[zz]).wait()
        out[...] += column[zz]
        return carry

    lax.fori_loop(1, Z, last, 0)

    def finish(k, carry):
        zz = (z + k) % Z
        for d in range(Q):
            to_c(zz, (q + d) % Q).wait_send()
        for d in range(1, Q):
            to_q(zz, (q + d) % Q).wait_send()
        return carry

    lax.fori_loop(0, Z, finish, 0)
    for d in range(1, Z):
        to_z((z + d) % Z).wait_send()


def scatter_sum(part, Z, L):
    rows = part.shape[-2]
    Q = 2 * L
    dma = pltpu.SemaphoreType.DMA
    return pl.pallas_call(
        functools.partial(scatter_kernel, Z, L),
        out_shape=jax.ShapeDtypeStruct((rows, LANES), jnp.float32),
        in_specs=[pl.BlockSpec(memory_space=pl.ANY)],
        out_specs=pl.BlockSpec(memory_space=pltpu.VMEM),
        scratch_shapes=[
            pltpu.VMEM((Q, Z, rows, LANES), jnp.bfloat16),
            pltpu.VMEM((Q, Z, rows, LANES), jnp.bfloat16),
            pltpu.VMEM((Z, Q, rows, LANES), jnp.bfloat16),
            pltpu.VMEM((Z, rows, LANES), jnp.float32),
            pltpu.VMEM((Z, rows, LANES), jnp.float32),
            dma((Q, Z)),
            dma((Q, Z)),
            dma((Q, Z)),
            dma((Q, Z)),
            dma((Z, Q)),
            dma((Z,)),
            dma((Z,)),
        ],
        compiler_params=pltpu.CompilerParams(
            collective_id=1, has_side_effects=True, vmem_limit_bytes=44 * 2**20
        ),
    )(part)


def on_device(
    Z, L, hidden_in, grad_heads, w_qkv, ln_gain, ln_bias, seq_lengths, sample_index, priority
):
    tok_rows, model_width = hidden_in.shape
    shard, qkv = w_qkv.shape
    padded = -(-shard // 16) * 16
    query_cols = QH * HD

    def whole(blocks):
        return blocks[..., :shard, :].reshape(model_width, LANES)

    def apart(rows):
        blocks = rows.reshape(L, Z, 2, 2, shard, LANES)
        return jnp.pad(blocks, ((0, 0),) * 4 + ((0, padded - shard), (0, 0)))

    own_block = jnp.concatenate([w_qkv, ln_gain[:, None], ln_bias[:, None]], axis=1)
    own_block = jnp.pad(own_block, ((0, padded - shard), (0, LANES - qkv - 2)))
    blocks, centre, variance = gather(own_block, hidden_in, Z, L)
    w_all = whole(blocks)
    picks = jnp.arange(16)[:, None] + qkv == jnp.arange(LANES)[None, :]
    picks = (picks & (jnp.arange(16) < 2)[:, None]).astype(jnp.bfloat16)
    contract = (((1,), (1,)), ((), ()))
    rows = lax.dot_general(picks, w_all, contract, preferred_element_type=jnp.float32)
    gain, bias = rows[0:1], rows[1:2]
    values = hidden_in.astype(jnp.float32)
    inverse = lax.rsqrt(variance[:, :1] + epsilon)
    normalized = (values - centre[:, :1]) * inverse
    normed = (normalized * gain + bias).astype(jnp.bfloat16)
    proj_total = jnp.dot(normed, w_all, preferred_element_type=jnp.float32)[:, :qkv]
    positions = lax.axis_index("local") * tok_rows + jnp.arange(tok_rows, dtype=jnp.int32)
    cosine, sine_table = rope_tables(positions, HD)
    query = rotate(proj_total[:, :query_cols].reshape(tok_rows, QH, HD), cosine, sine_table).astype(
        jnp.bfloat16
    )
    keys_own = rotate(proj_total[:, query_cols : query_cols + HD][:, None, :], cosine, sine_table)[
        :, 0, :
    ]
    pair_own = jnp.concatenate([keys_own, proj_total[:, query_cols + HD :]], axis=1).astype(
        jnp.bfloat16
    )
    def shifted_by(array, d):
        return lax.ppermute(array, "local", [(s, (s + d) % L) for s in range(L)])

    pair_all = jnp.concatenate([pair_own] + [shifted_by(pair_own, L - d) for d in range(1, L)])
    seq_rows = pair_all.shape[0]
    keys_all = pair_all[:, :HD]
    values_all = pair_all[:, HD:]
    length = seq_lengths[0]
    weight = lax.dynamic_slice(priority, (sample_index[0],), (1,))[0]
    scale = HD ** (-0.5)
    scores = jnp.einsum("qhd,kd->hqk", query, keys_all, preferred_element_type=jnp.float32) * scale
    key_positions = (
        lax.axis_index("local") * tok_rows + jnp.arange(seq_rows, dtype=jnp.int32)
    ) % seq_rows
    allowed = (key_positions[None, :] <= positions[:, None]) & (key_positions[None, :] < length)
    scores = jnp.where(allowed[None], scores, -1e30)
    row_max = jnp.max(scores, axis=-1, keepdims=True)
    exponent = jnp.exp(scores - row_max)
    attention = exponent / jnp.sum(exponent, axis=-1, keepdims=True)
    attention_b = attention.astype(jnp.bfloat16)
    head_out = jnp.einsum(
        "hqk,kd->qhd", attention_b, values_all, preferred_element_type=jnp.float32
    )
    live_rows = (positions < length).astype(jnp.float32)
    cotangent = (
        grad_heads.reshape(tok_rows, QH, HD).astype(jnp.float32) * weight * live_rows[:, None, None]
    ).astype(jnp.bfloat16)
    d_attention = jnp.einsum(
        "qhd,kd->hqk", cotangent, values_all, preferred_element_type=jnp.float32
    )
    row_delta = jnp.sum(cotangent.astype(jnp.float32) * head_out, axis=-1)
    d_scores = (attention * (d_attention - row_delta.T[:, :, None]) * scale).astype(jnp.bfloat16)
    d_query = jnp.einsum("hqk,kd->qhd", d_scores, keys_all, preferred_element_type=jnp.float32)
    d_key_term = jnp.einsum("hqk,qhd->kd", d_scores, query, preferred_element_type=jnp.float32)
    d_value_term = jnp.einsum(
        "hqk,qhd->kd", attention_b, cotangent, preferred_element_type=jnp.float32
    )
    d_pair_term = jnp.concatenate([d_key_term, d_value_term], axis=1)
    d_pair = d_pair_term[:tok_rows]
    for d in range(1, L):
        d_pair += shifted_by(d_pair_term[d * tok_rows : (d + 1) * tok_rows], d)
    d_query_pre = unrotate(d_query, cosine, sine_table).reshape(tok_rows, query_cols)
    d_key_pre = unrotate(d_pair[:, None, :HD], cosine, sine_table)[:, 0, :]
    d_projected = jnp.concatenate([d_query_pre, d_key_pre, d_pair[:, HD:]], axis=1)
    d_projected = jnp.pad(d_projected.astype(jnp.bfloat16), ((0, 0), (0, LANES - qkv)))
    d_normed = lax.dot_general(d_projected, w_all, contract, preferred_element_type=jnp.float32)
    grad_hat = d_normed * gain
    grad_input = inverse * (
        grad_hat
        - jnp.mean(grad_hat, axis=-1, keepdims=True)
        - normalized * jnp.mean(grad_hat * normalized, axis=-1, keepdims=True)
    )
    term_gain = jnp.sum(d_normed * normalized, axis=0, keepdims=True).astype(jnp.bfloat16)
    term_bias = jnp.sum(d_normed, axis=0, keepdims=True).astype(jnp.bfloat16)
    left = jnp.concatenate(
        [normed, term_gain, term_bias, jnp.zeros((14, model_width), jnp.bfloat16)], axis=0
    )
    right = jnp.concatenate([d_projected, picks], axis=0)
    term = lax.dot_general(
        left, right, (((0,), (0,)), ((), ())), preferred_element_type=jnp.float32
    ).astype(jnp.bfloat16)
    totals = scatter_sum(apart(term), Z, L)[:shard]
    return (
        grad_input.astype(jnp.bfloat16),
        totals[:, :qkv],
        totals[:, qkv],
        totals[:, qkv + 1],
    )


def solution(mesh):
    Z, L = mesh.shape["node"] // 4, mesh.shape["local"]
    return jax.shard_map(
        functools.partial(on_device, Z, L),
        mesh=mesh,
        in_specs=(
            P(("node", "local"), None),
            P(("node", "local"), None),
            P(("local", "node"), None),
            P(("local", "node")),
            P(("local", "node")),
            P("node"),
            P("node"),
            P(),
        ),
        out_specs=(
            P(("node", "local"), None),
            P(("local", "node"), None),
            P(("local", "node")),
            P(("local", "node")),
        ),
        check_vma=False,
    )
```

```python
import functools

import jax
import jax.numpy as jnp
from jax import lax
from jax.experimental import pallas as pl
from jax.experimental.pallas import tpu as pltpu
from jax.sharding import PartitionSpec as P

HD = 64
QH = 3
LANES = 384
MESH = pl.DeviceIdType.MESH


epsilon = 1e-05


def rope_tables(positions, head_size):
    half_size = head_size // 2
    steps = 2.0 * jnp.arange(half_size, dtype=jnp.float32) / head_size
    freqs = jnp.exp(-jnp.log(10000.0) * steps)
    angles = positions.astype(jnp.float32)[:, None] * freqs[None, :]
    cosine = jnp.concatenate([jnp.cos(angles), jnp.cos(angles)], axis=1)
    sine_table = jnp.concatenate([jnp.sin(angles), jnp.sin(angles)], axis=1)
    return (cosine, sine_table)


def rotate(values, cosine, sine_table):
    half_size = values.shape[-1] // 2
    turned = jnp.concatenate([-values[..., half_size:], values[..., :half_size]], axis=-1)
    return values * cosine[:, None, :] + turned * sine_table[:, None, :]


def unrotate(values, cosine, sine_table):
    half_size = values.shape[-1] // 2
    turned = jnp.concatenate([values[..., half_size:], -values[..., :half_size]], axis=-1)
    return values * cosine[:, None, :] + turned * sine_table[:, None, :]


def place(Z, L):
    node = lax.axis_index("node")
    z, x, c = node // 4, (node // 2) % 2, node % 2
    q = lax.axis_index("local") * 2 + x
    return z, q, c


def device(z, q, c):
    return (z * 4 + (q % 2) * 2 + c, q // 2)


def greet(Z, Q, z, q, c):
    barrier = pltpu.get_barrier_semaphore()

    def tell(target):
        pl.semaphore_signal(barrier, inc=1, device_id=target, device_id_type=MESH)

    tell(device(z, q, 1 - c))
    for d in range(1, Z):
        tell(device((z + d) % Z, q, c))
    for d in range(1, Q):
        tell(device(z, (q + d) % Q, c))
    pl.semaphore_wait(barrier, Z + Q - 1)


def gather_kernel(
    Z, L, own, hidden, out, centre, variance, held,
    local_sem, send_z, send_x, send_y, send_r0, send_r1, send_c,
    recv, recv_0, recv_1, recv_c,
):
    Q = 2 * L
    rows = own.shape[0]
    half = -(-(rows // 2) // 16) * 16
    z, q, c = place(Z, L)
    l, x = q // 2, q % 2
    greet(Z, Q, z, q, c)

    def block(zz, qq):
        return out.at[qq // 2, zz, qq % 2, c]

    def remote(src, dst, send, got, target):
        return pltpu.make_async_remote_copy(
            src_ref=src, dst_ref=dst, send_sem=send, recv_sem=got,
            device_id=target, device_id_type=MESH,
        )

    across = q + 1 - 2 * x

    def beside(d):
        return ((l + d) % L) * 2 + x

    mine = pltpu.make_async_copy(own, block(z, q), local_sem.at[0])
    mine.start()
    fetch = pltpu.make_async_copy(hidden, held, local_sem.at[1])
    fetch.start()

    def to_z(d):
        return remote(
            own, block(z, q), send_z.at[d - 1], recv.at[q, z], device((z + d) % Z, q, c)
        )

    def to_x(zz, src):
        return remote(src, block(zz, q), send_x.at[zz], recv.at[q, zz], device(z, across, c))

    def to_y(zz, d, src):
        return remote(
            src, block(zz, q), send_y.at[zz, d - 1], recv.at[q, zz], device(z, beside(d), c)
        )

    def relay_x(zz, d):
        part = block(zz, beside(d)).at[pl.ds(0, half)]
        return remote(
            part, part, send_r0.at[zz, d - 1], recv_0.at[beside(d), zz], device(z, across, c)
        )

    def relay_y(zz, d):
        part = block(zz, across).at[pl.ds(half, rows - half)]
        return remote(
            part, part, send_r1.at[zz, d - 1], recv_1.at[across, zz], device(z, beside(d), c)
        )

    def to_c(zz, qq, src):
        return remote(src, block(zz, qq), send_c.at[qq, zz], recv_c.at[qq, zz], device(z, q, 1 - c))

    def landed(zz, qq):
        pltpu.make_async_copy(own, block(zz, qq), recv.at[qq, zz]).wait()

    for d in range(1, Z):
        to_z(d).start()
    to_x(z, own).start()
    for d in range(1, L):
        to_y(z, d, own).start()
    to_c(z, q, own).start()

    fetch.wait()
    width = held.shape[1]

    def stats(g, carry):
        span = pl.ds(pl.multiple_of(g * 16, 16), 16)
        mean = jnp.sum(held[span, :].astype(jnp.float32), axis=1, keepdims=True) / width
        shifted = held[span, :].astype(jnp.float32) - mean
        spread_of = jnp.sum(shifted * shifted, axis=1, keepdims=True) / width
        centre[span, :] = jnp.broadcast_to(mean, (16, 128))
        variance[span, :] = jnp.broadcast_to(spread_of, (16, 128))
        return carry

    lax.fori_loop(0, held.shape[0] // 16, stats, 0)

    def spread(k):
        zz = (z + Z - k) % Z
        landed(zz, q)
        to_x(zz, block(zz, q)).start()
        for d in range(1, L):
            to_y(zz, d, block(zz, q)).start()
        to_c(zz, q, block(zz, q)).start()

    def relay(k):
        zz = (z + Z - k) % Z
        landed(zz, across)
        for d in range(1, L):
            relay_y(zz, d).start()
        to_c(zz, across, block(zz, across)).start()
        for d in range(1, L):
            landed(zz, beside(d))
            relay_x(zz, d).start()
            to_c(zz, beside(d), block(zz, beside(d))).start()

    def middle(k, carry):
        spread(k)
        relay(k - 1)
        return carry

    lax.fori_loop(1, Z, middle, 0)
    relay(Z - 1)

    def corners(k, carry):
        zz = (z + Z - k) % Z
        for d in range(1, L):
            qq = beside(d) + 1 - 2 * x
            at = block(zz, qq)
            low, high = pl.ds(0, half), pl.ds(half, rows - half)
            pltpu.make_async_copy(own.at[low], at.at[low], recv_0.at[qq, zz]).wait()
            pltpu.make_async_copy(own.at[high], at.at[high], recv_1.at[qq, zz]).wait()
            to_c(zz, qq, at).start()
        return carry

    lax.fori_loop(0, Z, corners, 0)

    mine.wait()
    for d in range(1, Z):
        to_z(d).wait_send()

    def finish(k, carry):
        to_x(k, own).wait_send()
        for d in range(1, L):
            to_y(k, d, own).wait_send()
            relay_x(k, d).wait_send()
            relay_y(k, d).wait_send()
        for d in range(Q):
            qq = (q + d) % Q
            to_c(k, qq, own).wait_send()
            pltpu.make_async_copy(own, out.at[qq // 2, k, qq % 2, 1 - c], recv_c.at[qq, k]).wait()
        return carry

    lax.fori_loop(0, Z, finish, 0)


def gather(block, hidden, Z, L):
    rows = block.shape[0]
    tokens = hidden.shape[0]
    Q = 2 * L
    dma = pltpu.SemaphoreType.DMA
    others = max(L - 1, 1)
    return pl.pallas_call(
        functools.partial(gather_kernel, Z, L),
        out_shape=(
            jax.ShapeDtypeStruct((L, Z, 2, 2, rows, LANES), jnp.bfloat16),
            jax.ShapeDtypeStruct((tokens, 128), jnp.float32),
            jax.ShapeDtypeStruct((tokens, 128), jnp.float32),
        ),
        in_specs=[pl.BlockSpec(memory_space=pl.ANY)] * 2,
        out_specs=(
            pl.BlockSpec(memory_space=pl.ANY),
            pl.BlockSpec(memory_space=pltpu.VMEM),
            pl.BlockSpec(memory_space=pltpu.VMEM),
        ),
        scratch_shapes=[
            pltpu.VMEM(hidden.shape, jnp.bfloat16),
            dma((2,)),
            dma((max(Z - 1, 1),)),
            dma((Z,)),
            dma((Z, others)),
            dma((Z, others)),
            dma((Z, others)),
            dma((Q, Z)),
            dma((Q, Z)),
            dma((Q, Z)),
            dma((Q, Z)),
            dma((Q, Z)),
        ],
        compiler_params=pltpu.CompilerParams(
            collective_id=0, has_side_effects=True, vmem_limit_bytes=32 * 2**20
        ),
    )(block, hidden)


def scatter_kernel(
    Z, L, part, vectors, out, own, pair, pair_vectors, packed, plane, tall, column,
    sem_own, sem_vectors, send_c, recv_c, send_q, recv_q, send_z, recv_z,
):
    Q = 2 * L
    rows = own.shape[2]
    half = rows // 2
    z, q, c = place(Z, L)
    greet(Z, Q, z, q, c)

    def load(zz, qq):
        return pltpu.make_async_copy(part.at[qq // 2, zz, qq % 2, c], own.at[qq, zz], sem_own.at[qq, zz])

    def to_c(zz, qq):
        return pltpu.make_async_remote_copy(
            src_ref=part.at[qq // 2, zz, qq % 2, 1 - c],
            dst_ref=pair.at[qq, zz],
            send_sem=send_c.at[qq, zz],
            recv_sem=recv_c.at[qq, zz],
            device_id=device(z, q, 1 - c),
            device_id_type=MESH,
        )

    def to_q(zz, qq):
        return pltpu.make_async_remote_copy(
            src_ref=packed.at[qq, zz],
            dst_ref=plane.at[zz, q],
            send_sem=send_q.at[qq, zz],
            recv_sem=recv_q.at[zz, q],
            device_id=device(z, qq, c),
            device_id_type=MESH,
        )

    def to_z(zz):
        return pltpu.make_async_remote_copy(
            src_ref=tall.at[zz],
            dst_ref=column.at[z],
            send_sem=send_z.at[zz],
            recv_sem=recv_z.at[z],
            device_id=device(zz, q, c),
            device_id_type=MESH,
        )

    other_vectors = pltpu.make_async_remote_copy(
        src_ref=vectors.at[1 - c],
        dst_ref=pair_vectors,
        send_sem=sem_vectors.at[0],
        recv_sem=sem_vectors.at[1],
        device_id=device(z, q, 1 - c),
        device_id_type=MESH,
    )
    other_vectors.start()

    def begin(k, carry):
        zz = (z + k) % Z
        for d in range(Q):
            qq = (q + d + 1) % Q
            to_c(zz, qq).start()
            load(zz, qq).start()
        return carry

    lax.fori_loop(1, Z + 1, begin, 0)

    def join(zz, qq):
        load(zz, qq).wait()
        to_c(zz, qq).wait_recv()
        def total(r, n, lane):
            at = (qq, zz, slice(r, r + n), slice(lane, lane + 128))
            return own[at].astype(jnp.float32) + pair[at].astype(jnp.float32)

        packed[qq, zz, 0:rows] = total(0, rows, 0).astype(jnp.bfloat16)
        packed[qq, zz, rows : 2 * rows] = total(0, rows, 128).astype(jnp.bfloat16)
        tail = total(0, rows, 256)
        tail = tail[:half] + pltpu.roll(tail[half:], 64, 1)
        ends = vectors[c, qq, zz] + pair_vectors[qq, zz]
        packed[qq, zz, 2 * rows :] = jnp.concatenate([tail, ends], axis=0).astype(jnp.bfloat16)

    def pairs(k):
        zz = (z + k) % Z

        def one(d, carry):
            qq = (q + d) % Q
            join(zz, qq)
            to_q(zz, qq).start()
            return carry

        lax.fori_loop(1, Q, one, 0)
        join(zz, q)

    other_vectors.wait()
    pairs(1)

    def plane_sum(zz):
        tall[zz] = packed[q, zz].astype(jnp.float32)

        def add(d, carry):
            qq = (q + d) % Q
            pltpu.make_async_copy(packed.at[qq, zz], plane.at[zz, qq], recv_q.at[zz, qq]).wait()
            tall[zz] += plane[zz, qq].astype(jnp.float32)
            return carry

        lax.fori_loop(1, Q, add, 0)

    def columns(k, carry):
        pairs(k + 1)
        zz = (z + k) % Z
        plane_sum(zz)
        to_z(zz).start()
        return carry

    lax.fori_loop(1, Z, columns, 0)
    plane_sum(z)
    out[...] = tall[z]

    def last(k, carry):
        zz = (z + Z - k) % Z
        pltpu.make_async_copy(tall.at[zz], column.at[zz], recv_z.at[zz]).wait()
        out[...] += column[zz]
        return carry

    lax.fori_loop(1, Z, last, 0)

    def finish(k, carry):
        zz = (z + k) % Z
        for d in range(Q):
            to_c(zz, (q + d) % Q).wait_send()
        for d in range(1, Q):
            to_q(zz, (q + d) % Q).wait_send()
        return carry

    lax.fori_loop(0, Z, finish, 0)
    for d in range(1, Z):
        to_z((z + d) % Z).wait_send()


def scatter_sum(part, vectors, Z, L):
    rows = part.shape[-2]
    ends = vectors.shape[-2]
    tall = 2 * rows + rows // 2 + ends
    Q = 2 * L
    dma = pltpu.SemaphoreType.DMA
    return pl.pallas_call(
        functools.partial(scatter_kernel, Z, L),
        out_shape=jax.ShapeDtypeStruct((tall, 128), jnp.float32),
        in_specs=[pl.BlockSpec(memory_space=pl.ANY), pl.BlockSpec(memory_space=pltpu.VMEM)],
        out_specs=pl.BlockSpec(memory_space=pltpu.VMEM),
        scratch_shapes=[
            pltpu.VMEM((Q, Z, rows, LANES), jnp.bfloat16),
            pltpu.VMEM((Q, Z, rows, LANES), jnp.bfloat16),
            pltpu.VMEM((Q, Z, ends, 128), jnp.float32),
            pltpu.VMEM((Q, Z, tall, 128), jnp.bfloat16),
            pltpu.VMEM((Z, Q, tall, 128), jnp.bfloat16),
            pltpu.VMEM((Z, tall, 128), jnp.float32),
            pltpu.VMEM((Z, tall, 128), jnp.float32),
            dma((Q, Z)),
            dma((2,)),
            dma((Q, Z)),
            dma((Q, Z)),
            dma((Q, Z)),
            dma((Z, Q)),
            dma((Z,)),
            dma((Z,)),
        ],
        compiler_params=pltpu.CompilerParams(
            collective_id=1, has_side_effects=True, vmem_limit_bytes=44 * 2**20
        ),
    )(part, vectors)


def on_device(
    Z, L, hidden_in, grad_heads, w_qkv, ln_gain, ln_bias, seq_lengths, sample_index, priority
):
    tok_rows, model_width = hidden_in.shape
    shard, qkv = w_qkv.shape
    padded = -(-shard // 16) * 16
    query_cols = QH * HD

    def whole(blocks):
        return blocks[..., :shard, :].reshape(model_width, LANES)

    def apart(rows):
        blocks = rows.reshape(L, Z, 2, 2, shard, LANES)
        return jnp.pad(blocks, ((0, 0),) * 4 + ((0, padded - shard), (0, 0)))

    own_block = jnp.concatenate([w_qkv, ln_gain[:, None], ln_bias[:, None]], axis=1)
    own_block = jnp.pad(own_block, ((0, padded - shard), (0, LANES - qkv - 2)))
    blocks, centre, variance = gather(own_block, hidden_in, Z, L)
    w_all = whole(blocks)
    picks = jnp.arange(16)[:, None] + qkv == jnp.arange(LANES)[None, :]
    picks = (picks & (jnp.arange(16) < 2)[:, None]).astype(jnp.bfloat16)
    contract = (((1,), (1,)), ((), ()))
    rows = lax.dot_general(picks, w_all, contract, preferred_element_type=jnp.float32)
    gain, bias = rows[0:1], rows[1:2]
    values = hidden_in.astype(jnp.float32)
    inverse = lax.rsqrt(variance[:, :1] + epsilon)
    normalized = (values - centre[:, :1]) * inverse
    normed = (normalized * gain + bias).astype(jnp.bfloat16)
    proj_total = jnp.dot(normed, w_all, preferred_element_type=jnp.float32)[:, :qkv]
    positions = lax.axis_index("local") * tok_rows + jnp.arange(tok_rows, dtype=jnp.int32)
    cosine, sine_table = rope_tables(positions, HD)
    query = rotate(proj_total[:, :query_cols].reshape(tok_rows, QH, HD), cosine, sine_table).astype(
        jnp.bfloat16
    )
    keys_own = rotate(proj_total[:, query_cols : query_cols + HD][:, None, :], cosine, sine_table)[
        :, 0, :
    ]
    pair_own = jnp.concatenate([keys_own, proj_total[:, query_cols + HD :]], axis=1).astype(
        jnp.bfloat16
    )
    def shifted_by(array, d):
        return lax.ppermute(array, "local", [(s, (s + d) % L) for s in range(L)])

    pair_all = jnp.concatenate([pair_own] + [shifted_by(pair_own, L - d) for d in range(1, L)])
    seq_rows = pair_all.shape[0]
    keys_all = pair_all[:, :HD]
    values_all = pair_all[:, HD:]
    length = seq_lengths[0]
    weight = lax.dynamic_slice(priority, (sample_index[0],), (1,))[0]
    scale = HD ** (-0.5)
    scores = jnp.einsum("qhd,kd->hqk", query, keys_all, preferred_element_type=jnp.float32) * scale
    key_positions = (
        lax.axis_index("local") * tok_rows + jnp.arange(seq_rows, dtype=jnp.int32)
    ) % seq_rows
    allowed = (key_positions[None, :] <= positions[:, None]) & (key_positions[None, :] < length)
    scores = jnp.where(allowed[None], scores, -1e30)
    row_max = jnp.max(scores, axis=-1, keepdims=True)
    exponent = jnp.exp(scores - row_max)
    attention = exponent / jnp.sum(exponent, axis=-1, keepdims=True)
    attention_b = attention.astype(jnp.bfloat16)
    head_out = jnp.einsum(
        "hqk,kd->qhd", attention_b, values_all, preferred_element_type=jnp.float32
    )
    live_rows = (positions < length).astype(jnp.float32)
    cotangent = (
        grad_heads.reshape(tok_rows, QH, HD).astype(jnp.float32) * weight * live_rows[:, None, None]
    ).astype(jnp.bfloat16)
    d_attention = jnp.einsum(
        "qhd,kd->hqk", cotangent, values_all, preferred_element_type=jnp.float32
    )
    row_delta = jnp.sum(cotangent.astype(jnp.float32) * head_out, axis=-1)
    d_scores = (attention * (d_attention - row_delta.T[:, :, None]) * scale).astype(jnp.bfloat16)
    d_query = jnp.einsum("hqk,kd->qhd", d_scores, keys_all, preferred_element_type=jnp.float32)
    d_key_term = jnp.einsum("hqk,qhd->kd", d_scores, query, preferred_element_type=jnp.float32)
    d_value_term = jnp.einsum(
        "hqk,qhd->kd", attention_b, cotangent, preferred_element_type=jnp.float32
    )
    d_pair_term = jnp.concatenate([d_key_term, d_value_term], axis=1)
    d_pair = d_pair_term[:tok_rows]
    for d in range(1, L):
        d_pair += shifted_by(d_pair_term[d * tok_rows : (d + 1) * tok_rows], d)
    d_query_pre = unrotate(d_query, cosine, sine_table).reshape(tok_rows, query_cols)
    d_key_pre = unrotate(d_pair[:, None, :HD], cosine, sine_table)[:, 0, :]
    d_projected = jnp.concatenate([d_query_pre, d_key_pre, d_pair[:, HD:]], axis=1)
    d_projected = jnp.pad(d_projected.astype(jnp.bfloat16), ((0, 0), (0, LANES - qkv)))
    d_normed = lax.dot_general(d_projected, w_all, contract, preferred_element_type=jnp.float32)
    grad_hat = d_normed * gain
    grad_input = inverse * (
        grad_hat
        - jnp.mean(grad_hat, axis=-1, keepdims=True)
        - normalized * jnp.mean(grad_hat * normalized, axis=-1, keepdims=True)
    )
    term_gain = jnp.sum(d_normed * normalized, axis=0, keepdims=True).astype(jnp.bfloat16)
    term_bias = jnp.sum(d_normed, axis=0, keepdims=True).astype(jnp.bfloat16)
    term = lax.dot_general(
        normed, d_projected, (((0,), (0,)), ((), ())), preferred_element_type=jnp.float32
    ).astype(jnp.bfloat16)
    lines = -(-shard // 128)
    ends = 2 * lines + (-(2 * lines + padded // 2)) % 16
    vectors = jnp.concatenate([term_gain, term_bias], axis=0).astype(jnp.float32)
    vectors = vectors.reshape(2, L, Z, 2, 2, shard).transpose(4, 1, 3, 2, 0, 5)
    vectors = jnp.pad(vectors, ((0, 0),) * 5 + ((0, lines * 128 - shard),))
    vectors = vectors.reshape(2, 2 * L, Z, 2 * lines, 128)
    vectors = jnp.pad(vectors, ((0, 0),) * 3 + ((0, ends - 2 * lines), (0, 0)))
    totals = scatter_sum(apart(term), vectors, Z, L)
    tail = totals[2 * padded : 2 * padded + padded // 2]
    tail = jnp.concatenate([tail[:, : HD], tail[:, HD:]], axis=0)
    first = 2 * padded + padded // 2
    return (
        grad_input.astype(jnp.bfloat16),
        jnp.concatenate([totals[:shard], totals[padded : padded + shard], tail[:shard]], axis=1),
        totals[first : first + lines].reshape(-1)[:shard],
        totals[first + lines : first + 2 * lines].reshape(-1)[:shard],
    )


def solution(mesh):
    Z, L = mesh.shape["node"] // 4, mesh.shape["local"]
    return jax.shard_map(
        functools.partial(on_device, Z, L),
        mesh=mesh,
        in_specs=(
            P(("node", "local"), None),
            P(("node", "local"), None),
            P(("local", "node"), None),
            P(("local", "node")),
            P(("local", "node")),
            P("node"),
            P("node"),
            P(),
        ),
        out_specs=(
            P(("node", "local"), None),
            P(("local", "node"), None),
            P(("local", "node")),
            P(("local", "node")),
        ),
        check_vma=False,
    )
```

```python
import functools

import jax
import jax.numpy as jnp
from jax import lax
from jax.experimental import pallas as pl
from jax.experimental.pallas import tpu as pltpu
from jax.sharding import PartitionSpec as P

HD = 64
QH = 3
LANES = 384
MESH = pl.DeviceIdType.MESH


epsilon = 1e-05


def rope_tables(positions, head_size):
    half_size = head_size // 2
    steps = 2.0 * jnp.arange(half_size, dtype=jnp.float32) / head_size
    freqs = jnp.exp(-jnp.log(10000.0) * steps)
    angles = positions.astype(jnp.float32)[:, None] * freqs[None, :]
    cosine = jnp.concatenate([jnp.cos(angles), jnp.cos(angles)], axis=1)
    sine_table = jnp.concatenate([jnp.sin(angles), jnp.sin(angles)], axis=1)
    return (cosine, sine_table)


def rotate(values, cosine, sine_table):
    half_size = values.shape[-1] // 2
    turned = jnp.concatenate([-values[..., half_size:], values[..., :half_size]], axis=-1)
    return values * cosine[:, None, :] + turned * sine_table[:, None, :]


def unrotate(values, cosine, sine_table):
    half_size = values.shape[-1] // 2
    turned = jnp.concatenate([values[..., half_size:], -values[..., :half_size]], axis=-1)
    return values * cosine[:, None, :] + turned * sine_table[:, None, :]


def place(Z, L):
    node = lax.axis_index("node")
    z, x, c = node // 4, (node // 2) % 2, node % 2
    q = lax.axis_index("local") * 2 + x
    return z, q, c


def device(z, q, c):
    return (z * 4 + (q % 2) * 2 + c, q // 2)


def greet(Z, Q, z, q, c):
    barrier = pltpu.get_barrier_semaphore()

    def tell(target):
        pl.semaphore_signal(barrier, inc=1, device_id=target, device_id_type=MESH)

    tell(device(z, q, 1 - c))
    for d in range(1, Z):
        tell(device((z + d) % Z, q, c))
    for d in range(1, Q):
        tell(device(z, (q + d) % Q, c))
    pl.semaphore_wait(barrier, Z + Q - 1)


def gather_kernel(
    Z, L, own, hidden, out, centre, variance, held,
    local_sem, send_z, send_x, send_y, send_r0, send_r1, send_c,
    recv, recv_0, recv_1, recv_c,
):
    Q = 2 * L
    rows = own.shape[0]
    half = -(-(rows // 2) // 16) * 16
    z, q, c = place(Z, L)
    l, x = q // 2, q % 2
    greet(Z, Q, z, q, c)

    def block(zz, qq):
        return out.at[qq // 2, zz, qq % 2, c]

    def remote(src, dst, send, got, target):
        return pltpu.make_async_remote_copy(
            src_ref=src, dst_ref=dst, send_sem=send, recv_sem=got,
            device_id=target, device_id_type=MESH,
        )

    across = q + 1 - 2 * x

    def beside(d):
        return ((l + d) % L) * 2 + x

    mine = pltpu.make_async_copy(own, block(z, q), local_sem.at[0])
    mine.start()
    fetch = pltpu.make_async_copy(hidden, held, local_sem.at[1])
    fetch.start()

    def to_z(d):
        return remote(
            own, block(z, q), send_z.at[d - 1], recv.at[q, z], device((z + d) % Z, q, c)
        )

    def to_x(zz, src):
        return remote(src, block(zz, q), send_x.at[zz], recv.at[q, zz], device(z, across, c))

    def to_y(zz, d, src):
        return remote(
            src, block(zz, q), send_y.at[zz, d - 1], recv.at[q, zz], device(z, beside(d), c)
        )

    def relay_x(zz, d):
        part = block(zz, beside(d)).at[pl.ds(0, half)]
        return remote(
            part, part, send_r0.at[zz, d - 1], recv_0.at[beside(d), zz], device(z, across, c)
        )

    def relay_y(zz, d):
        part = block(zz, across).at[pl.ds(half, rows - half)]
        return remote(
            part, part, send_r1.at[zz, d - 1], recv_1.at[across, zz], device(z, beside(d), c)
        )

    def to_c(zz, qq, src):
        return remote(src, block(zz, qq), send_c.at[qq, zz], recv_c.at[qq, zz], device(z, q, 1 - c))

    def landed(zz, qq):
        pltpu.make_async_copy(own, block(zz, qq), recv.at[qq, zz]).wait()

    for d in range(1, Z):
        to_z(d).start()
    to_x(z, own).start()
    for d in range(1, L):
        to_y(z, d, own).start()
    to_c(z, q, own).start()

    fetch.wait()
    width = held.shape[1]

    def stats(g, carry):
        span = pl.ds(pl.multiple_of(g * 16, 16), 16)
        mean = jnp.sum(held[span, :].astype(jnp.float32), axis=1, keepdims=True) / width
        shifted = held[span, :].astype(jnp.float32) - mean
        spread_of = jnp.sum(shifted * shifted, axis=1, keepdims=True) / width
        centre[span, :] = jnp.broadcast_to(mean, (16, 128))
        variance[span, :] = jnp.broadcast_to(spread_of, (16, 128))
        return carry

    lax.fori_loop(0, held.shape[0] // 16, stats, 0)

    def spread(k):
        zz = (z + Z - k) % Z
        landed(zz, q)
        to_x(zz, block(zz, q)).start()
        for d in range(1, L):
            to_y(zz, d, block(zz, q)).start()
        to_c(zz, q, block(zz, q)).start()

    def relay(k):
        zz = (z + Z - k) % Z
        landed(zz, across)
        for d in range(1, L):
            relay_y(zz, d).start()
        to_c(zz, across, block(zz, across)).start()
        for d in range(1, L):
            landed(zz, beside(d))
            relay_x(zz, d).start()
            to_c(zz, beside(d), block(zz, beside(d))).start()

    def middle(k, carry):
        spread(k)
        relay(k - 1)
        return carry

    lax.fori_loop(1, Z, middle, 0)
    relay(Z - 1)

    def corners(k, carry):
        zz = (z + Z - k) % Z
        for d in range(1, L):
            qq = beside(d) + 1 - 2 * x
            at = block(zz, qq)
            low, high = pl.ds(0, half), pl.ds(half, rows - half)
            pltpu.make_async_copy(own.at[low], at.at[low], recv_0.at[qq, zz]).wait()
            pltpu.make_async_copy(own.at[high], at.at[high], recv_1.at[qq, zz]).wait()
            to_c(zz, qq, at).start()
        return carry

    lax.fori_loop(0, Z, corners, 0)

    mine.wait()
    for d in range(1, Z):
        to_z(d).wait_send()

    def finish(k, carry):
        to_x(k, own).wait_send()
        for d in range(1, L):
            to_y(k, d, own).wait_send()
            relay_x(k, d).wait_send()
            relay_y(k, d).wait_send()
        for d in range(Q):
            qq = (q + d) % Q
            to_c(k, qq, own).wait_send()
            pltpu.make_async_copy(own, out.at[qq // 2, k, qq % 2, 1 - c], recv_c.at[qq, k]).wait()
        return carry

    lax.fori_loop(0, Z, finish, 0)


def gather(block, hidden, Z, L):
    rows = block.shape[0]
    tokens = hidden.shape[0]
    Q = 2 * L
    dma = pltpu.SemaphoreType.DMA
    others = max(L - 1, 1)
    return pl.pallas_call(
        functools.partial(gather_kernel, Z, L),
        out_shape=(
            jax.ShapeDtypeStruct((L, Z, 2, 2, rows, 128), jnp.bfloat16),
            jax.ShapeDtypeStruct((tokens, 128), jnp.float32),
            jax.ShapeDtypeStruct((tokens, 128), jnp.float32),
        ),
        in_specs=[pl.BlockSpec(memory_space=pl.ANY)] * 2,
        out_specs=(
            pl.BlockSpec(memory_space=pl.ANY),
            pl.BlockSpec(memory_space=pltpu.VMEM),
            pl.BlockSpec(memory_space=pltpu.VMEM),
        ),
        scratch_shapes=[
            pltpu.VMEM(hidden.shape, jnp.bfloat16),
            dma((2,)),
            dma((max(Z - 1, 1),)),
            dma((Z,)),
            dma((Z, others)),
            dma((Z, others)),
            dma((Z, others)),
            dma((Q, Z)),
            dma((Q, Z)),
            dma((Q, Z)),
            dma((Q, Z)),
            dma((Q, Z)),
        ],
        compiler_params=pltpu.CompilerParams(
            collective_id=0, has_side_effects=True, vmem_limit_bytes=32 * 2**20
        ),
    )(block, hidden)


def scatter_kernel(
    Z, L, part, vectors, out, own, pair, pair_vectors, packed, plane, tall, column,
    sem_own, sem_vectors, send_c, recv_c, send_q, recv_q, send_z, recv_z,
):
    Q = 2 * L
    rows = own.shape[2]
    half = rows // 2
    z, q, c = place(Z, L)
    greet(Z, Q, z, q, c)

    def load(zz, qq):
        return pltpu.make_async_copy(part.at[qq // 2, zz, qq % 2, c], own.at[qq, zz], sem_own.at[qq, zz])

    def to_c(zz, qq):
        return pltpu.make_async_remote_copy(
            src_ref=part.at[qq // 2, zz, qq % 2, 1 - c],
            dst_ref=pair.at[qq, zz],
            send_sem=send_c.at[qq, zz],
            recv_sem=recv_c.at[qq, zz],
            device_id=device(z, q, 1 - c),
            device_id_type=MESH,
        )

    def to_q(zz, qq):
        return pltpu.make_async_remote_copy(
            src_ref=packed.at[qq, zz],
            dst_ref=plane.at[zz, q],
            send_sem=send_q.at[qq, zz],
            recv_sem=recv_q.at[zz, q],
            device_id=device(z, qq, c),
            device_id_type=MESH,
        )

    def to_z(zz):
        return pltpu.make_async_remote_copy(
            src_ref=tall.at[zz],
            dst_ref=column.at[z],
            send_sem=send_z.at[zz],
            recv_sem=recv_z.at[z],
            device_id=device(zz, q, c),
            device_id_type=MESH,
        )

    other_vectors = pltpu.make_async_remote_copy(
        src_ref=vectors.at[1 - c],
        dst_ref=pair_vectors,
        send_sem=sem_vectors.at[0],
        recv_sem=sem_vectors.at[1],
        device_id=device(z, q, 1 - c),
        device_id_type=MESH,
    )
    other_vectors.start()

    def begin(k, carry):
        zz = (z + k) % Z
        for d in range(Q):
            qq = (q + d + 1) % Q
            to_c(zz, qq).start()
            load(zz, qq).start()
        return carry

    lax.fori_loop(1, Z + 1, begin, 0)

    def join(zz, qq):
        load(zz, qq).wait()
        to_c(zz, qq).wait_recv()
        def total(r, n, lane):
            at = (qq, zz, slice(r, r + n), slice(lane, lane + 128))
            return own[at].astype(jnp.float32) + pair[at].astype(jnp.float32)

        packed[qq, zz, 0:rows] = total(0, rows, 0).astype(jnp.bfloat16)
        packed[qq, zz, rows : 2 * rows] = total(0, rows, 128).astype(jnp.bfloat16)
        tail = total(0, rows, 256)
        tail = tail[:half] + pltpu.roll(tail[half:], 64, 1)
        ends = vectors[c, qq, zz] + pair_vectors[qq, zz]
        packed[qq, zz, 2 * rows :] = jnp.concatenate([tail, ends], axis=0).astype(jnp.bfloat16)

    def pairs(k):
        zz = (z + k) % Z

        def one(d, carry):
            qq = (q + d) % Q
            join(zz, qq)
            to_q(zz, qq).start()
            return carry

        lax.fori_loop(1, Q, one, 0)
        join(zz, q)

    other_vectors.wait()
    pairs(1)

    def plane_sum(zz):
        tall[zz] = packed[q, zz].astype(jnp.float32)

        def add(d, carry):
            qq = (q + d) % Q
            pltpu.make_async_copy(packed.at[qq, zz], plane.at[zz, qq], recv_q.at[zz, qq]).wait()
            tall[zz] += plane[zz, qq].astype(jnp.float32)
            return carry

        lax.fori_loop(1, Q, add, 0)

    def columns(k, carry):
        pairs(k + 1)
        zz = (z + k) % Z
        plane_sum(zz)
        to_z(zz).start()
        return carry

    lax.fori_loop(1, Z, columns, 0)
    plane_sum(z)
    out[...] = tall[z]

    def last(k, carry):
        zz = (z + Z - k) % Z
        pltpu.make_async_copy(tall.at[zz], column.at[zz], recv_z.at[zz]).wait()
        out[...] += column[zz]
        return carry

    lax.fori_loop(1, Z, last, 0)

    def finish(k, carry):
        zz = (z + k) % Z
        for d in range(Q):
            to_c(zz, (q + d) % Q).wait_send()
        for d in range(1, Q):
            to_q(zz, (q + d) % Q).wait_send()
        return carry

    lax.fori_loop(0, Z, finish, 0)
    for d in range(1, Z):
        to_z((z + d) % Z).wait_send()


def scatter_sum(part, vectors, Z, L):
    rows = part.shape[-2]
    ends = vectors.shape[-2]
    tall = 2 * rows + rows // 2 + ends
    Q = 2 * L
    dma = pltpu.SemaphoreType.DMA
    return pl.pallas_call(
        functools.partial(scatter_kernel, Z, L),
        out_shape=jax.ShapeDtypeStruct((tall, 128), jnp.float32),
        in_specs=[pl.BlockSpec(memory_space=pl.ANY), pl.BlockSpec(memory_space=pltpu.VMEM)],
        out_specs=pl.BlockSpec(memory_space=pltpu.VMEM),
        scratch_shapes=[
            pltpu.VMEM((Q, Z, rows, LANES), jnp.bfloat16),
            pltpu.VMEM((Q, Z, rows, LANES), jnp.bfloat16),
            pltpu.VMEM((Q, Z, ends, 128), jnp.float32),
            pltpu.VMEM((Q, Z, tall, 128), jnp.bfloat16),
            pltpu.VMEM((Z, Q, tall, 128), jnp.bfloat16),
            pltpu.VMEM((Z, tall, 128), jnp.float32),
            pltpu.VMEM((Z, tall, 128), jnp.float32),
            dma((Q, Z)),
            dma((2,)),
            dma((Q, Z)),
            dma((Q, Z)),
            dma((Q, Z)),
            dma((Z, Q)),
            dma((Z,)),
            dma((Z,)),
        ],
        compiler_params=pltpu.CompilerParams(
            collective_id=1, has_side_effects=True, vmem_limit_bytes=44 * 2**20
        ),
    )(part, vectors)


def on_device(
    Z, L, hidden_in, grad_heads, w_qkv, ln_gain, ln_bias, seq_lengths, sample_index, priority
):
    tok_rows, model_width = hidden_in.shape
    shard, qkv = w_qkv.shape
    padded = -(-shard // 16) * 16
    query_cols = QH * HD

    def apart(rows):
        blocks = rows.reshape(L, Z, 2, 2, shard, LANES)
        return jnp.pad(blocks, ((0, 0),) * 4 + ((0, padded - shard), (0, 0)))

    lines = -(-shard // HD)
    fold = -(-(padded + 2 * lines) // 32) * 16
    pair_rows = jnp.pad(jnp.stack([ln_gain, ln_bias]), ((0, 0), (0, lines * HD - shard)))
    pair_rows = pair_rows.reshape(2 * lines, HD)
    w_rows = jnp.pad(w_qkv, ((0, padded - shard), (0, 0)))
    narrow = jnp.concatenate([w_rows[:, 256:], pair_rows], axis=0)
    narrow = jnp.pad(narrow, ((0, 2 * fold - narrow.shape[0]), (0, 0)))
    narrow = jnp.concatenate([narrow[:fold], narrow[fold:]], axis=1)
    own_block = jnp.concatenate([w_rows[:, :128], w_rows[:, 128:256], narrow], axis=0)
    blocks, centre, variance = gather(own_block, hidden_in, Z, L)
    last = blocks[..., 2 * padded :, :]
    first_half, second_half = last[..., :HD], last[..., HD:]
    narrow = jnp.concatenate([first_half, second_half[..., : padded - fold, :]], axis=-2)
    w_all = jnp.concatenate(
        [blocks[..., :padded, :], blocks[..., padded : 2 * padded, :], narrow], axis=-1
    )
    w_all = w_all[..., :shard, :].reshape(model_width, qkv)
    ends = second_half[..., padded - fold : padded - fold + 2 * lines, :]
    ends = ends.reshape(L, Z, 2, 2, 2, lines * HD)[..., :shard].astype(jnp.float32)
    gain = ends[..., 0, :].reshape(1, model_width)
    bias = ends[..., 1, :].reshape(1, model_width)
    contract = (((1,), (1,)), ((), ()))
    values = hidden_in.astype(jnp.float32)
    inverse = lax.rsqrt(variance[:, :1] + epsilon)
    normalized = (values - centre[:, :1]) * inverse
    normed = (normalized * gain + bias).astype(jnp.bfloat16)
    proj_total = jnp.dot(normed, w_all, preferred_element_type=jnp.float32)
    positions = lax.axis_index("local") * tok_rows + jnp.arange(tok_rows, dtype=jnp.int32)
    cosine, sine_table = rope_tables(positions, HD)
    query = rotate(proj_total[:, :query_cols].reshape(tok_rows, QH, HD), cosine, sine_table).astype(
        jnp.bfloat16
    )
    keys_own = rotate(proj_total[:, query_cols : query_cols + HD][:, None, :], cosine, sine_table)[
        :, 0, :
    ]
    pair_own = jnp.concatenate([keys_own, proj_total[:, query_cols + HD :]], axis=1).astype(
        jnp.bfloat16
    )
    def shifted_by(array, d):
        return lax.ppermute(array, "local", [(s, (s + d) % L) for s in range(L)])

    pair_all = jnp.concatenate([pair_own] + [shifted_by(pair_own, L - d) for d in range(1, L)])
    seq_rows = pair_all.shape[0]
    keys_all = pair_all[:, :HD]
    values_all = pair_all[:, HD:]
    length = seq_lengths[0]
    weight = lax.dynamic_slice(priority, (sample_index[0],), (1,))[0]
    scale = HD ** (-0.5)
    scores = jnp.einsum("qhd,kd->hqk", query, keys_all, preferred_element_type=jnp.float32) * scale
    key_positions = (
        lax.axis_index("local") * tok_rows + jnp.arange(seq_rows, dtype=jnp.int32)
    ) % seq_rows
    allowed = (key_positions[None, :] <= positions[:, None]) & (key_positions[None, :] < length)
    scores = jnp.where(allowed[None], scores, -1e30)
    row_max = jnp.max(scores, axis=-1, keepdims=True)
    exponent = jnp.exp(scores - row_max)
    attention = exponent / jnp.sum(exponent, axis=-1, keepdims=True)
    attention_b = attention.astype(jnp.bfloat16)
    head_out = jnp.einsum(
        "hqk,kd->qhd", attention_b, values_all, preferred_element_type=jnp.float32
    )
    live_rows = (positions < length).astype(jnp.float32)
    cotangent = (
        grad_heads.reshape(tok_rows, QH, HD).astype(jnp.float32) * weight * live_rows[:, None, None]
    ).astype(jnp.bfloat16)
    d_attention = jnp.einsum(
        "qhd,kd->hqk", cotangent, values_all, preferred_element_type=jnp.float32
    )
    row_delta = jnp.sum(cotangent.astype(jnp.float32) * head_out, axis=-1)
    d_scores = (attention * (d_attention - row_delta.T[:, :, None]) * scale).astype(jnp.bfloat16)
    d_query = jnp.einsum("hqk,kd->qhd", d_scores, keys_all, preferred_element_type=jnp.float32)
    d_key_term = jnp.einsum("hqk,qhd->kd", d_scores, query, preferred_element_type=jnp.float32)
    d_value_term = jnp.einsum(
        "hqk,qhd->kd", attention_b, cotangent, preferred_element_type=jnp.float32
    )
    d_pair_term = jnp.concatenate([d_key_term, d_value_term], axis=1)
    d_pair = d_pair_term[:tok_rows]
    for d in range(1, L):
        d_pair += shifted_by(d_pair_term[d * tok_rows : (d + 1) * tok_rows], d)
    d_query_pre = unrotate(d_query, cosine, sine_table).reshape(tok_rows, query_cols)
    d_key_pre = unrotate(d_pair[:, None, :HD], cosine, sine_table)[:, 0, :]
    d_projected = jnp.concatenate([d_query_pre, d_key_pre, d_pair[:, HD:]], axis=1)
    d_projected = d_projected.astype(jnp.bfloat16)
    d_normed = lax.dot_general(d_projected, w_all, contract, preferred_element_type=jnp.float32)
    grad_hat = d_normed * gain
    grad_input = inverse * (
        grad_hat
        - jnp.mean(grad_hat, axis=-1, keepdims=True)
        - normalized * jnp.mean(grad_hat * normalized, axis=-1, keepdims=True)
    )
    term_gain = jnp.sum(d_normed * normalized, axis=0, keepdims=True).astype(jnp.bfloat16)
    term_bias = jnp.sum(d_normed, axis=0, keepdims=True).astype(jnp.bfloat16)
    d_padded = jnp.pad(d_projected, ((0, 0), (0, LANES - qkv)))
    term = lax.dot_general(
        normed, d_padded, (((0,), (0,)), ((), ())), preferred_element_type=jnp.float32
    ).astype(jnp.bfloat16)
    lines = -(-shard // 128)
    ends = 2 * lines + (-(2 * lines + padded // 2)) % 16
    vectors = jnp.concatenate([term_gain, term_bias], axis=0).astype(jnp.float32)
    vectors = vectors.reshape(2, L, Z, 2, 2, shard).transpose(4, 1, 3, 2, 0, 5)
    vectors = jnp.pad(vectors, ((0, 0),) * 5 + ((0, lines * 128 - shard),))
    vectors = vectors.reshape(2, 2 * L, Z, 2 * lines, 128)
    vectors = jnp.pad(vectors, ((0, 0),) * 3 + ((0, ends - 2 * lines), (0, 0)))
    totals = scatter_sum(apart(term), vectors, Z, L)
    tail = totals[2 * padded : 2 * padded + padded // 2]
    tail = jnp.concatenate([tail[:, : HD], tail[:, HD:]], axis=0)
    first = 2 * padded + padded // 2
    return (
        grad_input.astype(jnp.bfloat16),
        jnp.concatenate([totals[:shard], totals[padded : padded + shard], tail[:shard]], axis=1),
        totals[first : first + lines].reshape(-1)[:shard],
        totals[first + lines : first + 2 * lines].reshape(-1)[:shard],
    )


def solution(mesh):
    Z, L = mesh.shape["node"] // 4, mesh.shape["local"]
    return jax.shard_map(
        functools.partial(on_device, Z, L),
        mesh=mesh,
        in_specs=(
            P(("node", "local"), None),
            P(("node", "local"), None),
            P(("local", "node"), None),
            P(("local", "node")),
            P(("local", "node")),
            P("node"),
            P("node"),
            P(),
        ),
        out_specs=(
            P(("node", "local"), None),
            P(("local", "node"), None),
            P(("local", "node")),
            P(("local", "node")),
        ),
        check_vma=False,
    )
```

```python
import functools

import jax
import jax.numpy as jnp
from jax import lax
from jax.experimental import pallas as pl
from jax.experimental.pallas import tpu as pltpu
from jax.sharding import PartitionSpec as P

HD = 64
QH = 3
LANES = 384
MESH = pl.DeviceIdType.MESH


epsilon = 1e-05


def rope_tables(positions, head_size):
    half_size = head_size // 2
    steps = 2.0 * jnp.arange(half_size, dtype=jnp.float32) / head_size
    freqs = jnp.exp(-jnp.log(10000.0) * steps)
    angles = positions.astype(jnp.float32)[:, None] * freqs[None, :]
    cosine = jnp.concatenate([jnp.cos(angles), jnp.cos(angles)], axis=1)
    sine_table = jnp.concatenate([jnp.sin(angles), jnp.sin(angles)], axis=1)
    return (cosine, sine_table)


def rotate(values, cosine, sine_table):
    half_size = values.shape[-1] // 2
    turned = jnp.concatenate([-values[..., half_size:], values[..., :half_size]], axis=-1)
    return values * cosine[:, None, :] + turned * sine_table[:, None, :]


def unrotate(values, cosine, sine_table):
    half_size = values.shape[-1] // 2
    turned = jnp.concatenate([values[..., half_size:], -values[..., :half_size]], axis=-1)
    return values * cosine[:, None, :] + turned * sine_table[:, None, :]


def place(Z, L):
    node = lax.axis_index("node")
    z, x, c = node // 4, (node // 2) % 2, node % 2
    q = lax.axis_index("local") * 2 + x
    return z, q, c


def device(z, q, c):
    return (z * 4 + (q % 2) * 2 + c, q // 2)


def greet(Z, Q, z, q, c):
    barrier = pltpu.get_barrier_semaphore()

    def tell(target):
        pl.semaphore_signal(barrier, inc=1, device_id=target, device_id_type=MESH)

    tell(device(z, q, 1 - c))
    for d in range(1, Z):
        tell(device((z + d) % Z, q, c))
    for d in range(1, Q):
        tell(device(z, (q + d) % Q, c))
    pl.semaphore_wait(barrier, Z + Q - 1)


def gather_kernel(
    Z, L, own, hidden, out, centre, variance, held,
    local_sem, send_z, send_x, send_y, send_r0, send_r1, send_c,
    recv, recv_0, recv_1, recv_c,
):
    Q = 2 * L
    rows = own.shape[0]
    half = -(-(rows // 2) // 16) * 16
    z, q, c = place(Z, L)
    l, x = q // 2, q % 2
    greet(Z, Q, z, q, c)

    def block(zz, qq):
        return out.at[qq // 2, zz, qq % 2, c]

    def remote(src, dst, send, got, target):
        return pltpu.make_async_remote_copy(
            src_ref=src, dst_ref=dst, send_sem=send, recv_sem=got,
            device_id=target, device_id_type=MESH,
        )

    across = q + 1 - 2 * x

    def beside(d):
        return ((l + d) % L) * 2 + x

    mine = pltpu.make_async_copy(own, block(z, q), local_sem.at[0])
    mine.start()
    fetch = pltpu.make_async_copy(hidden, held, local_sem.at[1])
    fetch.start()

    def to_z(d):
        return remote(
            own, block(z, q), send_z.at[d - 1], recv.at[q, z], device((z + d) % Z, q, c)
        )

    def to_x(zz, src):
        return remote(src, block(zz, q), send_x.at[zz], recv.at[q, zz], device(z, across, c))

    def to_y(zz, d, src):
        return remote(
            src, block(zz, q), send_y.at[zz, d - 1], recv.at[q, zz], device(z, beside(d), c)
        )

    def relay_x(zz, d):
        part = block(zz, beside(d)).at[pl.ds(0, half)]
        return remote(
            part, part, send_r0.at[zz, d - 1], recv_0.at[beside(d), zz], device(z, across, c)
        )

    def relay_y(zz, d):
        part = block(zz, across).at[pl.ds(half, rows - half)]
        return remote(
            part, part, send_r1.at[zz, d - 1], recv_1.at[across, zz], device(z, beside(d), c)
        )

    def to_c(zz, qq, src):
        return remote(src, block(zz, qq), send_c.at[qq, zz], recv_c.at[qq, zz], device(z, q, 1 - c))

    def landed(zz, qq):
        pltpu.make_async_copy(own, block(zz, qq), recv.at[qq, zz]).wait()

    for d in range(1, Z):
        to_z(d).start()
    to_x(z, own).start()
    for d in range(1, L):
        to_y(z, d, own).start()
    to_c(z, q, own).start()

    fetch.wait()
    width = held.shape[1]

    def stats(g, carry):
        span = pl.ds(pl.multiple_of(g * 16, 16), 16)
        mean = jnp.sum(held[span, :].astype(jnp.float32), axis=1, keepdims=True) / width
        shifted = held[span, :].astype(jnp.float32) - mean
        spread_of = jnp.sum(shifted * shifted, axis=1, keepdims=True) / width
        centre[span, :] = jnp.broadcast_to(mean, (16, 128))
        variance[span, :] = jnp.broadcast_to(spread_of, (16, 128))
        return carry

    groups = held.shape[0] // 16

    def some_stats(k):
        lax.fori_loop(k * groups // Z, (k + 1) * groups // Z, stats, 0)

    def spread(k):
        zz = (z + Z - k) % Z
        landed(zz, q)
        to_x(zz, block(zz, q)).start()
        for d in range(1, L):
            to_y(zz, d, block(zz, q)).start()
        to_c(zz, q, block(zz, q)).start()

    def relay(k):
        zz = (z + Z - k) % Z
        landed(zz, across)
        for d in range(1, L):
            relay_y(zz, d).start()
        to_c(zz, across, block(zz, across)).start()
        for d in range(1, L):
            landed(zz, beside(d))
            relay_x(zz, d).start()
            to_c(zz, beside(d), block(zz, beside(d))).start()

    def middle(k, carry):
        spread(k)
        relay(k - 1)
        some_stats(k - 1)
        return carry

    lax.fori_loop(1, Z, middle, 0)
    relay(Z - 1)
    some_stats(Z - 1)

    def corners(k, carry):
        zz = (z + Z - k) % Z
        for d in range(1, L):
            qq = beside(d) + 1 - 2 * x
            at = block(zz, qq)
            low, high = pl.ds(0, half), pl.ds(half, rows - half)
            pltpu.make_async_copy(own.at[low], at.at[low], recv_0.at[qq, zz]).wait()
            pltpu.make_async_copy(own.at[high], at.at[high], recv_1.at[qq, zz]).wait()
            to_c(zz, qq, at).start()
        return carry

    lax.fori_loop(0, Z, corners, 0)

    mine.wait()
    for d in range(1, Z):
        to_z(d).wait_send()

    def finish(k, carry):
        to_x(k, own).wait_send()
        for d in range(1, L):
            to_y(k, d, own).wait_send()
            relay_x(k, d).wait_send()
            relay_y(k, d).wait_send()
        for d in range(Q):
            qq = (q + d) % Q
            to_c(k, qq, own).wait_send()
            pltpu.make_async_copy(own, out.at[qq // 2, k, qq % 2, 1 - c], recv_c.at[qq, k]).wait()
        return carry

    lax.fori_loop(0, Z, finish, 0)


def gather(block, hidden, Z, L):
    rows = block.shape[0]
    tokens = hidden.shape[0]
    Q = 2 * L
    dma = pltpu.SemaphoreType.DMA
    others = max(L - 1, 1)
    return pl.pallas_call(
        functools.partial(gather_kernel, Z, L),
        out_shape=(
            jax.ShapeDtypeStruct((L, Z, 2, 2, rows, 128), jnp.bfloat16),
            jax.ShapeDtypeStruct((tokens, 128), jnp.float32),
            jax.ShapeDtypeStruct((tokens, 128), jnp.float32),
        ),
        in_specs=[pl.BlockSpec(memory_space=pl.ANY)] * 2,
        out_specs=(
            pl.BlockSpec(memory_space=pl.ANY),
            pl.BlockSpec(memory_space=pltpu.VMEM),
            pl.BlockSpec(memory_space=pltpu.VMEM),
        ),
        scratch_shapes=[
            pltpu.VMEM(hidden.shape, jnp.bfloat16),
            dma((2,)),
            dma((max(Z - 1, 1),)),
            dma((Z,)),
            dma((Z, others)),
            dma((Z, others)),
            dma((Z, others)),
            dma((Q, Z)),
            dma((Q, Z)),
            dma((Q, Z)),
            dma((Q, Z)),
            dma((Q, Z)),
        ],
        compiler_params=pltpu.CompilerParams(
            collective_id=0, has_side_effects=True, vmem_limit_bytes=32 * 2**20
        ),
    )(block, hidden)


def scatter_kernel(
    Z, L, part, vectors, out, own, pair, pair_vectors, packed, plane, tall, column,
    sem_own, sem_vectors, send_c, recv_c, send_q, recv_q, send_z, recv_z,
):
    Q = 2 * L
    rows = own.shape[2]
    half = rows // 2
    z, q, c = place(Z, L)
    greet(Z, Q, z, q, c)

    def load(zz, qq):
        return pltpu.make_async_copy(part.at[qq // 2, zz, qq % 2, c], own.at[qq, zz], sem_own.at[qq, zz])

    def to_c(zz, qq):
        return pltpu.make_async_remote_copy(
            src_ref=part.at[qq // 2, zz, qq % 2, 1 - c],
            dst_ref=pair.at[qq, zz],
            send_sem=send_c.at[qq, zz],
            recv_sem=recv_c.at[qq, zz],
            device_id=device(z, q, 1 - c),
            device_id_type=MESH,
        )

    def to_q(zz, qq):
        return pltpu.make_async_remote_copy(
            src_ref=packed.at[qq, zz],
            dst_ref=plane.at[zz, q],
            send_sem=send_q.at[qq, zz],
            recv_sem=recv_q.at[zz, q],
            device_id=device(z, qq, c),
            device_id_type=MESH,
        )

    def to_z(zz):
        return pltpu.make_async_remote_copy(
            src_ref=tall.at[zz],
            dst_ref=column.at[z],
            send_sem=send_z.at[zz],
            recv_sem=recv_z.at[z],
            device_id=device(zz, q, c),
            device_id_type=MESH,
        )

    other_vectors = pltpu.make_async_remote_copy(
        src_ref=vectors.at[1 - c],
        dst_ref=pair_vectors,
        send_sem=sem_vectors.at[0],
        recv_sem=sem_vectors.at[1],
        device_id=device(z, q, 1 - c),
        device_id_type=MESH,
    )
    other_vectors.start()

    def begin(k, carry):
        zz = (z + k) % Z
        for d in range(Q):
            qq = (q + d + 1) % Q
            to_c(zz, qq).start()
            load(zz, qq).start()
        return carry

    lax.fori_loop(1, Z + 1, begin, 0)

    def join(zz, qq):
        load(zz, qq).wait()
        to_c(zz, qq).wait_recv()
        def total(r, n, lane):
            at = (qq, zz, slice(r, r + n), slice(lane, lane + 128))
            return own[at].astype(jnp.float32) + pair[at].astype(jnp.float32)

        packed[qq, zz, 0:rows] = total(0, rows, 0).astype(jnp.bfloat16)
        packed[qq, zz, rows : 2 * rows] = total(0, rows, 128).astype(jnp.bfloat16)
        tail = total(0, rows, 256)
        tail = tail[:half] + pltpu.roll(tail[half:], 64, 1)
        ends = vectors[c, qq, zz] + pair_vectors[qq, zz]
        packed[qq, zz, 2 * rows :] = jnp.concatenate([tail, ends], axis=0).astype(jnp.bfloat16)

    def pairs(k):
        zz = (z + k) % Z

        def one(d, carry):
            qq = (q + d) % Q
            join(zz, qq)
            to_q(zz, qq).start()
            return carry

        lax.fori_loop(1, Q, one, 0)
        join(zz, q)

    other_vectors.wait()
    pairs(1)

    def plane_sum(zz):
        tall[zz] = packed[q, zz].astype(jnp.float32)

        def add(d, carry):
            qq = (q + d) % Q
            pltpu.make_async_copy(packed.at[qq, zz], plane.at[zz, qq], recv_q.at[zz, qq]).wait()
            tall[zz] += plane[zz, qq].astype(jnp.float32)
            return carry

        lax.fori_loop(1, Q, add, 0)

    def columns(k, carry):
        pairs(k + 1)
        zz = (z + k) % Z
        plane_sum(zz)
        to_z(zz).start()
        return carry

    lax.fori_loop(1, Z, columns, 0)
    plane_sum(z)
    out[...] = tall[z]

    def last(k, carry):
        zz = (z + Z - k) % Z
        pltpu.make_async_copy(tall.at[zz], column.at[zz], recv_z.at[zz]).wait()
        out[...] += column[zz]
        return carry

    lax.fori_loop(1, Z, last, 0)

    def finish(k, carry):
        zz = (z + k) % Z
        for d in range(Q):
            to_c(zz, (q + d) % Q).wait_send()
        for d in range(1, Q):
            to_q(zz, (q + d) % Q).wait_send()
        return carry

    lax.fori_loop(0, Z, finish, 0)
    for d in range(1, Z):
        to_z((z + d) % Z).wait_send()


def scatter_sum(part, vectors, Z, L):
    rows = part.shape[-2]
    ends = vectors.shape[-2]
    tall = 2 * rows + rows // 2 + ends
    Q = 2 * L
    dma = pltpu.SemaphoreType.DMA
    return pl.pallas_call(
        functools.partial(scatter_kernel, Z, L),
        out_shape=jax.ShapeDtypeStruct((tall, 128), jnp.float32),
        in_specs=[pl.BlockSpec(memory_space=pl.ANY), pl.BlockSpec(memory_space=pltpu.VMEM)],
        out_specs=pl.BlockSpec(memory_space=pltpu.VMEM),
        scratch_shapes=[
            pltpu.VMEM((Q, Z, rows, LANES), jnp.bfloat16),
            pltpu.VMEM((Q, Z, rows, LANES), jnp.bfloat16),
            pltpu.VMEM((Q, Z, ends, 128), jnp.float32),
            pltpu.VMEM((Q, Z, tall, 128), jnp.bfloat16),
            pltpu.VMEM((Z, Q, tall, 128), jnp.bfloat16),
            pltpu.VMEM((Z, tall, 128), jnp.float32),
            pltpu.VMEM((Z, tall, 128), jnp.float32),
            dma((Q, Z)),
            dma((2,)),
            dma((Q, Z)),
            dma((Q, Z)),
            dma((Q, Z)),
            dma((Z, Q)),
            dma((Z,)),
            dma((Z,)),
        ],
        compiler_params=pltpu.CompilerParams(
            collective_id=1, has_side_effects=True, vmem_limit_bytes=44 * 2**20
        ),
    )(part, vectors)


def on_device(
    Z, L, hidden_in, grad_heads, w_qkv, ln_gain, ln_bias, seq_lengths, sample_index, priority
):
    tok_rows, model_width = hidden_in.shape
    shard, qkv = w_qkv.shape
    padded = -(-shard // 16) * 16
    query_cols = QH * HD

    def apart(rows):
        blocks = rows.reshape(L, Z, 2, 2, shard, LANES)
        return jnp.pad(blocks, ((0, 0),) * 4 + ((0, padded - shard), (0, 0)))

    lines = -(-shard // HD)
    fold = -(-(padded + 2 * lines) // 32) * 16
    pair_rows = jnp.pad(jnp.stack([ln_gain, ln_bias]), ((0, 0), (0, lines * HD - shard)))
    pair_rows = pair_rows.reshape(2 * lines, HD)
    w_rows = jnp.pad(w_qkv, ((0, padded - shard), (0, 0)))
    narrow = jnp.concatenate([w_rows[:, 256:], pair_rows], axis=0)
    narrow = jnp.pad(narrow, ((0, 2 * fold - narrow.shape[0]), (0, 0)))
    narrow = jnp.concatenate([narrow[:fold], narrow[fold:]], axis=1)
    own_block = jnp.concatenate([w_rows[:, :128], w_rows[:, 128:256], narrow], axis=0)
    blocks, centre, variance = gather(own_block, hidden_in, Z, L)
    last = blocks[..., 2 * padded :, :]
    first_half, second_half = last[..., :HD], last[..., HD:]
    narrow = jnp.concatenate([first_half, second_half[..., : padded - fold, :]], axis=-2)
    w_all = jnp.concatenate(
        [blocks[..., :padded, :], blocks[..., padded : 2 * padded, :], narrow], axis=-1
    )
    w_all = w_all[..., :shard, :].reshape(model_width, qkv)
    ends = second_half[..., padded - fold : padded - fold + 2 * lines, :]
    ends = ends.reshape(L, Z, 2, 2, 2, lines * HD)[..., :shard].astype(jnp.float32)
    gain = ends[..., 0, :].reshape(1, model_width)
    bias = ends[..., 1, :].reshape(1, model_width)
    contract = (((1,), (1,)), ((), ()))
    values = hidden_in.astype(jnp.float32)
    inverse = lax.rsqrt(variance[:, :1] + epsilon)
    normalized = (values - centre[:, :1]) * inverse
    normed = (normalized * gain + bias).astype(jnp.bfloat16)
    proj_total = jnp.dot(normed, w_all, preferred_element_type=jnp.float32)
    positions = lax.axis_index("local") * tok_rows + jnp.arange(tok_rows, dtype=jnp.int32)
    cosine, sine_table = rope_tables(positions, HD)
    query = rotate(proj_total[:, :query_cols].reshape(tok_rows, QH, HD), cosine, sine_table).astype(
        jnp.bfloat16
    )
    keys_own = rotate(proj_total[:, query_cols : query_cols + HD][:, None, :], cosine, sine_table)[
        :, 0, :
    ]
    pair_own = jnp.concatenate([keys_own, proj_total[:, query_cols + HD :]], axis=1).astype(
        jnp.bfloat16
    )
    def shifted_by(array, d):
        return lax.ppermute(array, "local", [(s, (s + d) % L) for s in range(L)])

    pair_all = jnp.concatenate([pair_own] + [shifted_by(pair_own, L - d) for d in range(1, L)])
    seq_rows = pair_all.shape[0]
    keys_all = pair_all[:, :HD]
    values_all = pair_all[:, HD:]
    length = seq_lengths[0]
    weight = lax.dynamic_slice(priority, (sample_index[0],), (1,))[0]
    scale = HD ** (-0.5)
    scores = jnp.einsum("qhd,kd->hqk", query, keys_all, preferred_element_type=jnp.float32) * scale
    key_positions = (
        lax.axis_index("local") * tok_rows + jnp.arange(seq_rows, dtype=jnp.int32)
    ) % seq_rows
    allowed = (key_positions[None, :] <= positions[:, None]) & (key_positions[None, :] < length)
    scores = jnp.where(allowed[None], scores, -1e30)
    row_max = jnp.max(scores, axis=-1, keepdims=True)
    exponent = jnp.exp(scores - row_max)
    attention = exponent / jnp.sum(exponent, axis=-1, keepdims=True)
    attention_b = attention.astype(jnp.bfloat16)
    head_out = jnp.einsum(
        "hqk,kd->qhd", attention_b, values_all, preferred_element_type=jnp.float32
    )
    live_rows = (positions < length).astype(jnp.float32)
    cotangent = (
        grad_heads.reshape(tok_rows, QH, HD).astype(jnp.float32) * weight * live_rows[:, None, None]
    ).astype(jnp.bfloat16)
    d_attention = jnp.einsum(
        "qhd,kd->hqk", cotangent, values_all, preferred_element_type=jnp.float32
    )
    row_delta = jnp.sum(cotangent.astype(jnp.float32) * head_out, axis=-1)
    d_scores = (attention * (d_attention - row_delta.T[:, :, None]) * scale).astype(jnp.bfloat16)
    d_query = jnp.einsum("hqk,kd->qhd", d_scores, keys_all, preferred_element_type=jnp.float32)
    d_key_term = jnp.einsum("hqk,qhd->kd", d_scores, query, preferred_element_type=jnp.float32)
    d_value_term = jnp.einsum(
        "hqk,qhd->kd", attention_b, cotangent, preferred_element_type=jnp.float32
    )
    d_pair_term = jnp.concatenate([d_key_term, d_value_term], axis=1)
    d_pair = d_pair_term[:tok_rows]
    for d in range(1, L):
        d_pair += shifted_by(d_pair_term[d * tok_rows : (d + 1) * tok_rows], d)
    d_query_pre = unrotate(d_query, cosine, sine_table).reshape(tok_rows, query_cols)
    d_key_pre = unrotate(d_pair[:, None, :HD], cosine, sine_table)[:, 0, :]
    d_projected = jnp.concatenate([d_query_pre, d_key_pre, d_pair[:, HD:]], axis=1)
    d_projected = d_projected.astype(jnp.bfloat16)
    d_normed = lax.dot_general(d_projected, w_all, contract, preferred_element_type=jnp.float32)
    grad_hat = d_normed * gain
    grad_input = inverse * (
        grad_hat
        - jnp.mean(grad_hat, axis=-1, keepdims=True)
        - normalized * jnp.mean(grad_hat * normalized, axis=-1, keepdims=True)
    )
    term_gain = jnp.sum(d_normed * normalized, axis=0, keepdims=True).astype(jnp.bfloat16)
    term_bias = jnp.sum(d_normed, axis=0, keepdims=True).astype(jnp.bfloat16)
    d_padded = jnp.pad(d_projected, ((0, 0), (0, LANES - qkv)))
    term = lax.dot_general(
        normed, d_padded, (((0,), (0,)), ((), ())), preferred_element_type=jnp.float32
    ).astype(jnp.bfloat16)
    lines = -(-shard // 128)
    ends = 2 * lines + (-(2 * lines + padded // 2)) % 16
    vectors = jnp.concatenate([term_gain, term_bias], axis=0).astype(jnp.float32)
    vectors = vectors.reshape(2, L, Z, 2, 2, shard).transpose(4, 1, 3, 2, 0, 5)
    vectors = jnp.pad(vectors, ((0, 0),) * 5 + ((0, lines * 128 - shard),))
    vectors = vectors.reshape(2, 2 * L, Z, 2 * lines, 128)
    vectors = jnp.pad(vectors, ((0, 0),) * 3 + ((0, ends - 2 * lines), (0, 0)))
    totals = scatter_sum(apart(term), vectors, Z, L)
    tail = totals[2 * padded : 2 * padded + padded // 2]
    tail = jnp.concatenate([tail[:, : HD], tail[:, HD:]], axis=0)
    first = 2 * padded + padded // 2
    return (
        grad_input.astype(jnp.bfloat16),
        jnp.concatenate([totals[:shard], totals[padded : padded + shard], tail[:shard]], axis=1),
        totals[first : first + lines].reshape(-1)[:shard],
        totals[first + lines : first + 2 * lines].reshape(-1)[:shard],
    )


def solution(mesh):
    Z, L = mesh.shape["node"] // 4, mesh.shape["local"]
    return jax.shard_map(
        functools.partial(on_device, Z, L),
        mesh=mesh,
        in_specs=(
            P(("node", "local"), None),
            P(("node", "local"), None),
            P(("local", "node"), None),
            P(("local", "node")),
            P(("local", "node")),
            P("node"),
            P("node"),
            P(),
        ),
        out_specs=(
            P(("node", "local"), None),
            P(("local", "node"), None),
            P(("local", "node")),
            P(("local", "node")),
        ),
        check_vma=False,
    )
```
